256 devices in a mesh: row: 16 (over z, y_lo), col: 4 (over x), ch: 4 (over y_hi, core).
Axes of the slice: x: 4, y: 4 (y_hi: 2, y_lo: 2; y = y_hi * 2 + y_lo), z: 8, core: 2. Of those that a mesh axis runs over, the one named last changes fastest.
Arguments:
- pair: float32 [1024, 1024, 128], P('row', ('col', 'ch')), may hold values from -30 to 30
- token_mask: int32 [1024], replicated, may hold values 0 or 1
- in_gain: float32 [2, 128], replicated, may hold values from 0.1 to 1.9
- in_bias: float32 [2, 128], replicated, may hold values from -3 to 3
- proj_weight: bfloat16 [2, 128, 512], replicated, may hold values from -0.5 to 0.5
- gate_weight: bfloat16 [2, 128, 128], replicated, may hold values from -0.5 to 0.5
- mid_gain: float32 [2, 128], replicated, may hold values from 0.1 to 1.9
- mid_bias: float32 [2, 128], replicated, may hold values from -3 to 3
- out_weight: bfloat16 [2, 128, 128], replicated, may hold values from -0.5 to 0.5
Outputs:
- new_pair: float32 [1024, 1024, 128], P('row', ('col', 'ch'))
The draws below stay inside these ranges and needn't reach their ends.
All inputs are finite; a program needn't handle non-finite values.
Results may differ from the reference program's by a relative error of at most 0.0022.
Values may be sent and summed in bfloat16 or wider, within the bound.
No kernel may reach another device: no remote copies, remote signals or barrier semaphores. Data moves between devices by JAX's collectives and lax.ppermute only.
A program may use at most 192 MiB of HBM per device.

```python
import jax
import jax.numpy as jnp
from jax import lax

C = 128
N = 1024


def draw_pair(key, part):
    key = jax.random.fold_in(key, 11)
    first, second, third = jax.random.split(key, 3)
    row_scale = jnp.exp(jax.random.uniform(first, (N, 1, 1), jnp.float32) * jnp.log(10.0))
    col_scale = jnp.exp(jax.random.uniform(second, (1, N, 1), jnp.float32) * jnp.log(10.0))
    scales = jnp.sqrt(row_scale * col_scale)
    values = jax.random.normal(third, (N, N, C), jnp.float32) * scales
    return jnp.clip(values, -30.0, 30.0).astype(jnp.float32)


def touch_ends(array, stream_key, smallest, largest):
    place = [jax.random.randint(jax.random.fold_in(stream_key, axis), (), 0, length) for axis, length in enumerate(array.shape)]
    main_axis = array.shape.index(max(array.shape))
    beside = place[:main_axis] + [(place[main_axis] + 1) % array.shape[main_axis]] + place[main_axis + 1:]
    return array.at[tuple(place)].set(smallest).at[tuple(beside)].set(largest)


def noise(stream_key, dims, scale, most, kind=jnp.bfloat16):
    return jnp.clip(scale * jax.random.normal(stream_key, dims, jnp.float32), -most, most).astype(kind)


def setup_inputs(seed: int = 0) -> dict:
    streams_of = jax.random.split(jax.random.key(seed), 10)
    return {
        "pair": draw_pair(jax.random.fold_in(streams_of[9], 71), 0),
        "token_mask": touch_ends((jax.random.randint(streams_of[1], (N,), 0, 8) < 7).astype(jnp.int32), jax.random.fold_in(streams_of[1], 1), 0, 1),
        "in_gain": jnp.clip(1.0 + 0.18 * jax.random.normal(streams_of[2], (2, C), jnp.float32), 0.1, 1.9),
        "in_bias": noise(streams_of[3], (2, C), 0.5, 3.0, jnp.float32),
        "proj_weight": noise(streams_of[4], (2, C, 4 * C), C ** -0.5, 0.5),
        "gate_weight": noise(streams_of[5], (2, C, C), C ** -0.5, 0.5),
        "mid_gain": jnp.clip(1.0 + 0.18 * jax.random.normal(streams_of[6], (2, C), jnp.float32), 0.1, 1.9),
        "mid_bias": noise(streams_of[7], (2, C), 0.5, 3.0, jnp.float32),
        "out_weight": noise(streams_of[8], (2, C, C), C ** -0.5, 0.5),
    }


def layer_norm(values, scale_by, shift_by, along):
    average = lax.optimization_barrier(jnp.mean(values, axis=along, keepdims=True))
    centred = values - average
    spread = lax.optimization_barrier(jnp.mean(centred * centred, axis=along, keepdims=True))
    return centred * lax.rsqrt(spread + 1e-05) * scale_by + shift_by

def reference(pair, token_mask, in_gain, in_bias, proj_weight, gate_weight, mid_gain, mid_bias, out_weight):
    token_float = token_mask.astype(jnp.float32)
    pair_mask = token_float[:, None] * token_float[None, :]
    current = pair
    for section in range(2):
        normed = layer_norm(current, in_gain[section], in_bias[section], 2).astype(jnp.bfloat16)
        normed_wide = normed.astype(jnp.float32)
        weights = proj_weight[section].astype(jnp.float32)

        def side(offset):
            gate_part = jnp.einsum('ijc,cd->dij', normed_wide, weights[:, offset:offset + C])
            value_part = jnp.einsum('ijc,cd->dij', normed_wide, weights[:, offset + C:offset + 2 * C])
            return (jax.nn.sigmoid(gate_part) * value_part * pair_mask[None]).astype(jnp.bfloat16)
        left_block = side(0).astype(jnp.float32)
        right_block = side(2 * C).astype(jnp.float32)
        gate_values = jax.nn.sigmoid(jnp.einsum('ijc,cd->ijd', normed_wide, gate_weight[section].astype(jnp.float32)))
        if section == 0:
            triangle = jnp.einsum('cik,cjk->cij', left_block, right_block)
        else:
            triangle = jnp.einsum('cki,ckj->cij', left_block, right_block)
        normed_mid = layer_norm(triangle, mid_gain[section][:, None, None], mid_bias[section][:, None, None], 0).astype(jnp.bfloat16)
        update_values = jnp.einsum('cij,cd->ijd', normed_mid.astype(jnp.float32), out_weight[section].astype(jnp.float32))
        current = current + gate_values * update_values
    return current
```

```python
import jax
import jax.numpy as jnp
from jax import lax
from jax.experimental import pallas as pl
from jax.experimental.pallas import tpu as pltpu
from jax.sharding import PartitionSpec as P

F32 = jnp.float32
BF16 = jnp.bfloat16
C = 128
T = 64
H = 32
BLK = 16
VMEM_LIMIT = 40 * 1024 * 1024


def sigmoid(x):
    return 0.5 * jnp.tanh(0.5 * x) + 0.5


def layer_norm(values, gain, bias):
    average = jnp.mean(values, axis=-1, keepdims=True)
    centred = values - average
    spread = jnp.mean(centred * centred, axis=-1, keepdims=True)
    return centred * lax.rsqrt(spread + 1e-05) * gain + bias


def project_block(load, block, mask_ref, gain, bias, w_ref, g_ref, x_ref, gate_ref, sl_ref, sr_ref):
    for t in range(0, BLK, 2):
        s = block * BLK + t
        lines = jnp.concatenate([load(s), load(s + H), load(s + 1), load(s + 1 + H)], axis=0)
        normed = layer_norm(lines, gain, bias).astype(BF16)
        p = lax.dot_general(
            w_ref[...], normed, (((0,), (1,)), ((), ())), preferred_element_type=F32
        )
        gate = sigmoid(jnp.dot(normed, g_ref[...], preferred_element_type=F32))
        gate_ref[s] = gate[:C]
        gate_ref[s + 1] = gate[C:]
        left = sigmoid(p[:C]) * p[C : 2 * C]
        right = sigmoid(p[2 * C : 3 * C]) * p[3 * C :]
        for u in range(2):
            mask = mask_ref[pl.ds(s + u, 1), :]
            sl_ref[:, t + u, :] = left[:, u * C : (u + 1) * C] * mask
            sr_ref[:, t + u, :] = right[:, u * C : (u + 1) * C] * mask
    x_ref[:, pl.ds(pl.multiple_of(block * BLK, BLK), BLK), :] = sl_ref[...].astype(BF16)
    x_ref[:, pl.ds(pl.multiple_of(H + block * BLK, BLK), BLK), :] = sr_ref[...].astype(BF16)


def first_kernel(z_ref, mask_ref, gain_ref, bias_ref, w_ref, g_ref, x_ref, gate_ref, sl_ref, sr_ref):
    gain, bias = gain_ref[...], bias_ref[...]

    def body(block, carry):
        project_block(
            lambda s: z_ref[s], block, mask_ref, gain, bias, w_ref, g_ref, x_ref, gate_ref, sl_ref, sr_ref
        )
        return carry

    lax.fori_loop(0, H // BLK, body, 0)


def update_block(block, y_ref, gain, bias, ow_ref, gate_ref, s_ref, emit):
    y = y_ref[:, pl.ds(pl.multiple_of(block * BLK, BLK), BLK), :].astype(F32)
    average = jnp.sum(y, axis=0) * (1.0 / C)
    centred = y - average[None]
    spread = jnp.sum(centred * centred, axis=0) * (1.0 / C)
    s_ref[...] = centred * lax.rsqrt(spread + 1e-05)[None]
    for t in range(BLK):
        s = block * BLK + t
        normed = (s_ref[:, t, :] * gain + bias).astype(BF16)
        update = lax.dot_general(
            normed, ow_ref[...], (((0,), (0,)), ((), ())), preferred_element_type=F32
        )
        emit(s, gate_ref[s] * update)


def middle_kernel(
    y_ref, z_ref, gate0_ref, mgain_ref, mbias_ref, ow_ref, mask_ref, gain_ref, bias_ref, w_ref, g_ref,
    x_ref, gate_ref, zn_ref, sl_ref, sr_ref,
):
    mgain, mbias = mgain_ref[...], mbias_ref[...]
    gain, bias = gain_ref[...], bias_ref[...]

    def emit(s, change):
        zn_ref[s] = z_ref[s] + change[:T]
        zn_ref[s + H] = z_ref[s + H] + change[T:]

    def body(block, carry):
        update_block(block, y_ref, mgain, mbias, ow_ref, gate0_ref, sl_ref, emit)
        return carry

    lax.fori_loop(0, H // BLK, body, 0)

    for block in range(H // BLK):
        project_block(
            lambda s: zn_ref[:, s, :], block, mask_ref, gain, bias, w_ref, g_ref, x_ref, gate_ref, sl_ref, sr_ref
        )


def last_kernel(y_ref, z_ref, gate_ref, mgain_ref, mbias_ref, ow_ref, out_ref, s_ref):
    mgain, mbias = mgain_ref[...], mbias_ref[...]

    def emit(s, change):
        out_ref[:, s, :] = z_ref[:, s, :] + change[:T]
        out_ref[:, s + H, :] = z_ref[:, s + H, :] + change[T:]

    for block in range(H // BLK):
        update_block(block, y_ref, mgain, mbias, ow_ref, gate_ref, s_ref, emit)


def sides(x0, x1):
    low = jnp.concatenate([x0[:, :T], x1[:, :T]], axis=1)
    high = jnp.concatenate([x0[:, T:], x1[:, T:]], axis=1)
    return low, high


def nt_dot(a, b):
    return lax.dot_general(a, b, (((1,), (1,)), ((), ())), preferred_element_type=F32)


def outgoing_kernel(x_ref, l_ref, r_ref, other_ref, rs_ref):
    core = lax.axis_index("core")

    def gather(row, carry):
        at = pl.multiple_of(row * T, T)
        to = pl.multiple_of(lax.rem(row, 2) * 512 + lax.div(row, 2) * T, T)
        for q in range(4):
            low, high = sides(x_ref[row * 8 + 2 * q], x_ref[row * 8 + 2 * q + 1])
            cols = slice(q * 128, (q + 1) * 128)
            l_ref[pl.ds(at, H), cols] = low[:H]
            l_ref[pl.ds(at + H, H), cols] = high[:H]
            rs_ref[pl.ds(to, H), cols] = low[H:]
            rs_ref[pl.ds(to + H, H), cols] = high[H:]
        return carry

    lax.fori_loop(0, 16, gather, 0)
    r_ref[...] = rs_ref[pl.ds(pl.multiple_of(core * 512, 512), 512), :]
    send = rs_ref[pl.ds(pl.multiple_of((1 - core) * 512, 512), 512), :]

    def multiply(i, carry):
        rows = pl.ds(pl.multiple_of(i * 256, 256), 256)
        other_ref[rows, :] = nt_dot(l_ref[rows, :], send).astype(BF16)
        return carry

    lax.fori_loop(0, 4, multiply, 0)


def outgoing_sum_kernel(l_ref, r_ref, got_ref, y_ref):
    def body(i, carry):
        rows = pl.ds(pl.multiple_of(i * 256, 256), 256)
        total = (nt_dot(l_ref[rows, :], r_ref[...]) + got_ref[rows, :].astype(F32)).astype(BF16)
        for b in range(4):
            row = i * 4 + b
            for q in range(4):
                part = total[b * T : (b + 1) * T, q * 128 : (q + 1) * 128]
                first, second = sides(part[:H], part[H:])
                y_ref[row * 8 + 2 * q] = first
                y_ref[row * 8 + 2 * q + 1] = second
        return carry

    lax.fori_loop(0, 4, body, 0)


def incoming_kernel(x_ref, l_ref, r_ref):
    def gather(c, carry):
        at = pl.multiple_of(c * T, T)
        for q in range(8):
            low, high = sides(x_ref[16 * q + c], x_ref[16 * q + 8 + c])
            cols = slice(q * 128, (q + 1) * 128)
            l_ref[pl.ds(at, H), cols] = low[:H]
            l_ref[pl.ds(at + H, H), cols] = high[:H]
            r_ref[pl.ds(at, H), cols] = low[H:]
            r_ref[pl.ds(at + H, H), cols] = high[H:]
        return carry

    lax.fori_loop(0, 8, gather, 0)


def incoming_sum_kernel(l_ref, r_ref, got_ref, y_ref):
    core = lax.axis_index("core")

    def body(i, carry):
        right = r_ref[pl.ds(pl.multiple_of(i * 128, 128), 128), :]
        for left_ref, parity in ((l_ref, core), (got_ref, 1 - core)):
            total = nt_dot(right, left_ref[...]).astype(BF16)
            for b in range(2):
                c = i * 2 + b
                for q in range(4):
                    part = total[b * T : (b + 1) * T, q * 128 : (q + 1) * 128]
                    first, second = sides(part[:H], part[H:])
                    y_ref[(4 * q + parity) * 8 + c] = first
                    y_ref[(4 * q + 2 + parity) * 8 + c] = second
        return carry

    lax.fori_loop(0, 4, body, 0)


def call(kernel, outs, scratch=(), flops=0, moved=0):
    return pl.pallas_call(
        kernel,
        out_shape=[jax.ShapeDtypeStruct(s, d) for s, d in outs],
        scratch_shapes=[pltpu.VMEM(s, d) for s, d in scratch],
        compiler_params=pltpu.CompilerParams(vmem_limit_bytes=VMEM_LIMIT),
        cost_estimate=pl.CostEstimate(flops=flops, bytes_accessed=moved, transcendentals=0),
    )


CHIPS = ("row", "col", "yh")
SWAP = ((0, 1), (1, 0))


def exchange(x):
    return lax.all_to_all(x, CHIPS, split_axis=0, concat_axis=0, tiled=True)


def on_device(
    pair, token_mask, in_gain, in_bias, proj_weight, gate_weight, mid_gain, mid_bias, out_weight
):
    row = lax.axis_index("row")
    block = lax.axis_index("col") * 4 + lax.axis_index("yh") * 2 + lax.axis_index("core")
    row_mask = lax.dynamic_slice_in_dim(token_mask, row * T, T).astype(F32)
    col_mask = lax.dynamic_slice_in_dim(token_mask, block * T, T).astype(F32)
    mask0 = (row_mask.reshape(2, H).T[:, :, None] * col_mask).reshape(H, 2 * T)
    mask1 = (col_mask.reshape(2, H).T[:, :, None] * row_mask).reshape(H, 2 * T)
    gates = ((H, 2 * T, C), F32)
    wide = ((C, T, 2 * T), BF16)
    narrow = ((C, H, 2 * T), BF16)
    line = ((C, BLK, 2 * T), F32)

    x, gate0 = call(first_kernel, [wide, gates], [line, line])(
        pair, mask0, in_gain[:1], in_bias[:1], proj_weight[0], gate_weight[0]
    )
    x = exchange(x)
    left, right, other = call(
        outgoing_kernel,
        [((1024, 512), BF16), ((512, 512), BF16), ((1024, 512), BF16)],
        [((1024, 512), BF16)],
    )(x)
    got = lax.ppermute(other, "core", SWAP)
    (y,) = call(outgoing_sum_kernel, [narrow])(left, right, got)
    y = exchange(y)
    x, gate1, current = call(middle_kernel, [wide, gates, ((T, T, C), F32)], [line, line])(
        y, pair, gate0, mid_gain[0][:, None], mid_bias[0][:, None], out_weight[0],
        mask1, in_gain[1:], in_bias[1:], proj_weight[1], gate_weight[1],
    )
    x = exchange(x)
    left, right = call(incoming_kernel, [((512, 1024), BF16), ((512, 1024), BF16)])(x)
    got = lax.ppermute(left, "core", SWAP)
    (y,) = call(incoming_sum_kernel, [narrow])(left, right, got)
    y = exchange(y)
    (out,) = call(last_kernel, [((T, T, C), F32)], [line])(
        y, current, gate1, mid_gain[1][:, None], mid_bias[1][:, None], out_weight[1]
    )
    return out


def solution(mesh):
    inner = jax.sharding.Mesh(mesh.devices.reshape(16, 4, 2, 2), ("row", "col", "yh", "core"))
    spec = P("row", ("col", "yh", "core"), None)
    return jax.shard_map(
        on_device,
        mesh=inner,
        in_specs=(spec, P(), P(), P(), P(), P(), P(), P(), P()),
        out_specs=spec,
        check_vma=False,
    )
```

```python
import jax
import jax.numpy as jnp
from jax import lax
from jax.experimental import pallas as pl
from jax.experimental.pallas import tpu as pltpu
from jax.sharding import PartitionSpec as P

F32 = jnp.float32
BF16 = jnp.bfloat16
C = 128
T = 64
H = 32
BLK = 16
VMEM_LIMIT = 24 * 1024 * 1024
FIRST_LIMIT = 56 * 1024 * 1024


def sigmoid(x):
    return 0.5 * jnp.tanh(0.5 * x) + 0.5


def layer_norm(values, gain, bias):
    average = jnp.mean(values, axis=-1, keepdims=True)
    centred = values - average
    spread = jnp.mean(centred * centred, axis=-1, keepdims=True)
    return centred * lax.rsqrt(spread + 1e-05) * gain + bias


def lanes_twice(mask_ref, block):
    chunk = mask_ref[:, pl.ds(pl.multiple_of(lax.div(block, 2) * 2 * T, 2 * T), 2 * T)].astype(F32)
    turned = jnp.concatenate([chunk[:, T:], chunk[:, :T]], axis=1)
    lane = lax.broadcasted_iota(jnp.int32, (1, 2 * T), 1)
    keep = lax.div(lane, T) == lax.rem(block, 2)
    return jnp.where(keep, chunk, turned)


def line_mask(token_ref, start, s, across):
    lane = lax.broadcasted_iota(jnp.int32, (1, 2 * T), 1)
    first, second = token_ref[start + s].astype(F32), token_ref[start + s + H].astype(F32)
    return jnp.where(lane < T, first, second) * across


def row_block():
    return lax.axis_index("z") * 2 + lax.axis_index("yl")


def col_block():
    return lax.axis_index("x") * 4 + lax.axis_index("yh") * 2 + lax.axis_index("core")


def column(row):
    shape = (C, C)
    eye = lax.broadcasted_iota(jnp.int32, shape, 0) == lax.broadcasted_iota(jnp.int32, shape, 1)
    return jnp.sum(jnp.where(eye, jnp.broadcast_to(row, shape), 0.0), axis=1, keepdims=True)


def project_block(load, block, mask, gain, bias, w, g, x_ref, gate_ref, sl_ref, sr_ref):
    for t in range(0, BLK, 2):
        s = block * BLK + t
        lines = jnp.concatenate([load(s), load(s + H), load(s + 1), load(s + 1 + H)], axis=0)
        normed = layer_norm(lines, gain, bias).astype(BF16)
        p = lax.dot_general(
            w, normed, (((0,), (1,)), ((), ())), preferred_element_type=F32
        )
        gate = sigmoid(jnp.dot(normed, g, preferred_element_type=F32))
        gate_ref[s] = gate[:C]
        gate_ref[s + 1] = gate[C:]
        left = sigmoid(p[:C]) * p[C : 2 * C]
        right = sigmoid(p[2 * C : 3 * C]) * p[3 * C :]
        for u in range(2):
            keep = mask(s + u)
            sl_ref[:, t + u, :] = left[:, u * C : (u + 1) * C] * keep
            sr_ref[:, t + u, :] = right[:, u * C : (u + 1) * C] * keep
    x_ref[:, pl.ds(pl.multiple_of(block * BLK, BLK), BLK), :] = sl_ref[...].astype(BF16)
    x_ref[:, pl.ds(pl.multiple_of(H + block * BLK, BLK), BLK), :] = sr_ref[...].astype(BF16)


def first_kernel(
    z_hbm, token_hbm, mask_hbm, gain_hbm, bias_hbm, w_hbm, g_hbm, x_hbm, gate_hbm, sl_ref, sr_ref,
    z_ref, token_ref, mask_ref, gain_ref, bias_ref, w_ref, g_ref, x_ref, gate_ref, small_sem, z_sem, out_sem,
):
    small = [
        pltpu.make_async_copy(source, to, small_sem.at[n])
        for n, (source, to) in enumerate(
            (
                (gain_hbm, gain_ref), (bias_hbm, bias_ref), (mask_hbm, mask_ref), (token_hbm, token_ref),
                (w_hbm.at[0], w_ref), (g_hbm.at[0], g_ref),
            )
        )
    ]
    parts = []
    for block in range(H // BLK):
        for half in range(2):
            lines = pl.ds(half * H + block * BLK, BLK)
            parts.append(pltpu.make_async_copy(z_hbm.at[lines], z_ref.at[lines], z_sem.at[len(parts)]))
    for copy in small + parts:
        copy.start()
    for copy in small:
        copy.wait()
    gain, bias = gain_ref[0:1], bias_ref[0:1]
    across = lanes_twice(mask_ref, col_block())
    start = row_block() * T
    copies = []
    for block in range(H // BLK):
        parts[2 * block].wait()
        parts[2 * block + 1].wait()
        project_block(
            lambda s: z_ref[s], block, lambda s: line_mask(token_ref, start, s, across), gain, bias,
            w_ref[...], g_ref[...], x_ref, gate_ref, sl_ref, sr_ref,
        )
        for half in range(2):
            lines = pl.ds(half * H + block * BLK, BLK)
            copies.append(
                pltpu.make_async_copy(x_ref.at[:, lines], x_hbm.at[:, lines], out_sem.at[len(copies)])
            )
            copies[-1].start()
        lines = pl.ds(block * BLK, BLK)
        copies.append(pltpu.make_async_copy(gate_ref.at[lines], gate_hbm.at[lines], out_sem.at[len(copies)]))
        copies[-1].start()
    for copy in copies:
        copy.wait()


def update_block(block, y_ref, gain, bias, ow, gate_ref, s_ref, emit):
    y = y_ref[:, pl.ds(pl.multiple_of(block * BLK, BLK), BLK), :].astype(F32)
    average = jnp.sum(y, axis=0) * (1.0 / C)
    centred = y - average[None]
    spread = jnp.sum(centred * centred, axis=0) * (1.0 / C)
    s_ref[...] = centred * lax.rsqrt(spread + 1e-05)[None]
    for t in range(BLK):
        s = block * BLK + t
        normed = (s_ref[:, t, :] * gain + bias).astype(BF16)
        update = lax.dot_general(
            normed, ow, (((0,), (0,)), ((), ())), preferred_element_type=F32
        )
        emit(s, gate_ref[s] * update)


def middle_kernel(
    y_ref, z_ref, gate0_ref, mgain_ref, mbias_ref, ow_ref, token_ref, mask_ref, gain_ref, bias_ref,
    w_ref, g_ref, x_ref, gate_ref, zn_ref, sl_ref, sr_ref,
):
    mgain, mbias = column(mgain_ref[0:1]), column(mbias_ref[0:1])
    gain, bias = gain_ref[1:2], bias_ref[1:2]
    across = lanes_twice(mask_ref, row_block())
    start = col_block() * T

    def emit(s, change):
        zn_ref[s] = z_ref[s] + change[:T]
        zn_ref[s + H] = z_ref[s + H] + change[T:]

    def body(block, carry):
        update_block(block, y_ref, mgain, mbias, ow_ref[0], gate0_ref, sl_ref, emit)
        return carry

    lax.fori_loop(0, H // BLK, body, 0)

    for block in range(H // BLK):
        project_block(
            lambda s: zn_ref[:, s, :], block, lambda s: line_mask(token_ref, start, s, across), gain, bias,
            w_ref[1], g_ref[1], x_ref, gate_ref, sl_ref, sr_ref,
        )


def last_kernel(y_ref, z_ref, gate_ref, mgain_ref, mbias_ref, ow_ref, out_ref, s_ref):
    mgain, mbias = column(mgain_ref[1:2]), column(mbias_ref[1:2])

    def emit(s, change):
        out_ref[:, s, :] = z_ref[:, s, :] + change[:T]
        out_ref[:, s + H, :] = z_ref[:, s + H, :] + change[T:]

    for block in range(H // BLK):
        update_block(block, y_ref, mgain, mbias, ow_ref[1], gate_ref, s_ref, emit)


def sides(x0, x1):
    low = jnp.concatenate([x0[:, :T], x1[:, :T]], axis=1)
    high = jnp.concatenate([x0[:, T:], x1[:, T:]], axis=1)
    return low, high


def nt_dot(a, b):
    return lax.dot_general(a, b, (((1,), (1,)), ((), ())), preferred_element_type=F32)


def chip(row, col):
    return lax.div(row, 2) * 16 + lax.rem(col, 2) * 8 + lax.rem(row, 2) * 4 + lax.div(col, 2)


def outgoing_kernel(x_ref, l_ref, r_ref, other_ref, rs_ref):
    core = lax.axis_index("core")

    def gather(row, carry):
        at = pl.multiple_of(row * T, T)
        to = pl.multiple_of(lax.rem(row, 2) * 512 + lax.div(row, 2) * T, T)
        base = chip(row, 0)
        for q in range(4):
            low, high = sides(x_ref[base + q], x_ref[base + 8 + q])
            cols = slice(q * 128, (q + 1) * 128)
            l_ref[pl.ds(at, H), cols] = low[:H]
            l_ref[pl.ds(at + H, H), cols] = high[:H]
            rs_ref[pl.ds(to, H), cols] = low[H:]
            rs_ref[pl.ds(to + H, H), cols] = high[H:]
        return carry

    lax.fori_loop(0, 16, gather, 0)
    r_ref[...] = rs_ref[pl.ds(pl.multiple_of(core * 512, 512), 512), :]
    send = rs_ref[pl.ds(pl.multiple_of((1 - core) * 512, 512), 512), :]

    def multiply(i, carry):
        rows = pl.ds(pl.multiple_of(i * 256, 256), 256)
        other_ref[rows, :] = nt_dot(l_ref[rows, :], send).astype(BF16)
        return carry

    lax.fori_loop(0, 4, multiply, 0)


def outgoing_sum_kernel(l_ref, r_ref, got_ref, y_ref):
    def body(i, carry):
        rows = pl.ds(pl.multiple_of(i * 256, 256), 256)
        total = (nt_dot(l_ref[rows, :], r_ref[...]) + got_ref[rows, :].astype(F32)).astype(BF16)
        for b in range(4):
            base = chip(i * 4 + b, 0)
            for q in range(4):
                part = total[b * T : (b + 1) * T, q * 128 : (q + 1) * 128]
                first, second = sides(part[:H], part[H:])
                y_ref[base + q] = first
                y_ref[base + 8 + q] = second
        return carry

    lax.fori_loop(0, 4, body, 0)


def incoming_kernel(x_ref, l_ref, r_ref):
    def gather(c, carry):
        at = pl.multiple_of(c * T, T)
        base = chip(0, c)
        for q in range(8):
            low, high = sides(x_ref[16 * q + base], x_ref[16 * q + 4 + base])
            cols = slice(q * 128, (q + 1) * 128)
            l_ref[pl.ds(at, H), cols] = low[:H]
            l_ref[pl.ds(at + H, H), cols] = high[:H]
            r_ref[pl.ds(at, H), cols] = low[H:]
            r_ref[pl.ds(at + H, H), cols] = high[H:]
        return carry

    lax.fori_loop(0, 8, gather, 0)


def incoming_half(l_ref, r_ref, write):
    def body(i, carry):
        right = r_ref[pl.ds(pl.multiple_of(i * 128, 128), 128), :]
        total = nt_dot(right, l_ref[...]).astype(BF16)
        for b in range(2):
            base = chip(0, i * 2 + b)
            for q in range(4):
                part = total[b * T : (b + 1) * T, q * 128 : (q + 1) * 128]
                first, second = sides(part[:H], part[H:])
                write(2 * q, base, first)
                write(2 * q + 1, base, second)
        return carry

    lax.fori_loop(0, 4, body, 0)


def incoming_own_kernel(l_ref, r_ref, half_ref):
    def write(plane, base, value):
        half_ref[plane * 16 + base] = value

    incoming_half(l_ref, r_ref, write)


def incoming_sum_kernel(l_ref, r_ref, half_ref, y_ref):
    own = lax.axis_index("core")

    def write(plane, base, value):
        y_ref[plane * 16 + (1 - own) * 4 + base] = value

    incoming_half(l_ref, r_ref, write)
    for plane in range(8):
        for y in range(2):
            y_ref[pl.ds(plane * 16 + y * 8 + own * 4, 4)] = half_ref[pl.ds(plane * 16 + y * 8, 4)]


def call(kernel, outs, scratch=(), specs=None, out_specs=None, limit=VMEM_LIMIT):
    return pl.pallas_call(
        kernel,
        out_shape=[jax.ShapeDtypeStruct(s, d) for s, d in outs],
        scratch_shapes=[pltpu.VMEM(*m) if isinstance(m, tuple) else m for m in scratch],
        compiler_params=pltpu.CompilerParams(vmem_limit_bytes=limit),
        **({} if specs is None else {"in_specs": specs}),
        **({} if out_specs is None else {"out_specs": out_specs}),
    )


VMEM_SPEC = pl.BlockSpec(memory_space=pltpu.VMEM)
SMEM_SPEC = pl.BlockSpec(memory_space=pltpu.SMEM)
HBM_SPEC = pl.BlockSpec(memory_space=pltpu.HBM)
CHIPS = ("z", "yh", "yl", "x")
SWAP = ((0, 1), (1, 0))


def exchange(x):
    return lax.all_to_all(x, CHIPS, split_axis=0, concat_axis=0, tiled=True)


def on_device(
    pair, token_mask, in_gain, in_bias, proj_weight, gate_weight, mid_gain, mid_bias, out_weight
):
    mask = token_mask[None]
    gates = ((H, 2 * T, C), F32)
    wide = ((C, T, 2 * T), BF16)
    narrow = ((C, H, 2 * T), BF16)
    line = ((C, BLK, 2 * T), F32)

    x, gate0 = call(
        first_kernel,
        [wide, gates],
        [
            line, line, ((T, T, C), F32), pltpu.SMEM((1024,), jnp.int32), ((1, 1024), jnp.int32), ((2, C), F32),
            ((2, C), F32), ((C, 4 * C), BF16), ((C, C), BF16), wide, gates, pltpu.SemaphoreType.DMA((6,)),
            pltpu.SemaphoreType.DMA((4,)), pltpu.SemaphoreType.DMA((6,)),
        ],
        [HBM_SPEC] * 7,
        [HBM_SPEC] * 2,
        FIRST_LIMIT,
    )(
        pair, token_mask, mask, in_gain, in_bias, proj_weight, gate_weight
    )
    x = exchange(x)
    left, right, other = call(
        outgoing_kernel,
        [((1024, 512), BF16), ((512, 512), BF16), ((1024, 512), BF16)],
        [((1024, 512), BF16)],
    )(x)
    got = lax.ppermute(other, "core", SWAP)
    (y,) = call(outgoing_sum_kernel, [narrow])(left, right, got)
    y = exchange(y)
    x, gate1, current = call(middle_kernel, [wide, gates, ((T, T, C), F32)], [line, line], [VMEM_SPEC] * 6 + [SMEM_SPEC] + [VMEM_SPEC] * 5)(
        y, pair, gate0, mid_gain, mid_bias, out_weight,
        token_mask, mask, in_gain, in_bias, proj_weight, gate_weight,
    )
    x = exchange(x)
    left, right = call(incoming_kernel, [((512, 1024), BF16), ((512, 1024), BF16)])(x)
    got = lax.ppermute(left, "core", SWAP)
    (half,) = call(incoming_own_kernel, [narrow])(left, right)
    (y,) = call(incoming_sum_kernel, [narrow])(got, right, half)
    y = exchange(y)
    (out,) = call(last_kernel, [((T, T, C), F32)], [line])(
        y, current, gate1, mid_gain, mid_bias, out_weight
    )
    return out


def solution(mesh):
    inner = jax.sharding.Mesh(mesh.devices.reshape(8, 2, 4, 2, 2), ("z", "yl", "x", "yh", "core"))
    spec = P(("z", "yl"), ("x", "yh", "core"), None)
    return jax.shard_map(
        on_device,
        mesh=inner,
        in_specs=(spec, P(), P(), P(), P(), P(), P(), P(), P()),
        out_specs=spec,
        check_vma=False,
    )
```

```python
import jax
import jax.numpy as jnp
from jax import lax
from jax.experimental import pallas as pl
from jax.experimental.pallas import tpu as pltpu
from jax.sharding import PartitionSpec as P

F32 = jnp.float32
BF16 = jnp.bfloat16
C = 128
T = 64
H = 32
PITCH = 24
WIDE = 72
BLK = 16
VMEM_LIMIT = 24 * 1024 * 1024
FIRST_LIMIT = 56 * 1024 * 1024


def sigmoid(x):
    return 0.5 * jnp.tanh(0.5 * x) + 0.5


def layer_norm(values, gain, bias):
    average = jnp.mean(values, axis=-1, keepdims=True)
    centred = values - average
    spread = jnp.mean(centred * centred, axis=-1, keepdims=True)
    return centred * lax.rsqrt(spread + 1e-05) * gain + bias


def lanes_twice(mask_ref, block):
    chunk = mask_ref[:, pl.ds(pl.multiple_of(lax.div(block, 2) * 2 * T, 2 * T), 2 * T)].astype(F32)
    turned = jnp.concatenate([chunk[:, T:], chunk[:, :T]], axis=1)
    lane = lax.broadcasted_iota(jnp.int32, (1, 2 * T), 1)
    keep = lax.div(lane, T) == lax.rem(block, 2)
    return jnp.where(keep, chunk, turned)


def line_mask(token_ref, start, s, across):
    lane = lax.broadcasted_iota(jnp.int32, (1, 2 * T), 1)
    first, second = token_ref[start + s].astype(F32), token_ref[start + s + H].astype(F32)
    return jnp.where(lane < T, first, second) * across


def row_block():
    return lax.axis_index("z") * 2 + lax.axis_index("yl")


def col_block():
    return lax.axis_index("x") * 4 + lax.axis_index("yh") * 2 + lax.axis_index("core")


def column(row):
    shape = (C, C)
    eye = lax.broadcasted_iota(jnp.int32, shape, 0) == lax.broadcasted_iota(jnp.int32, shape, 1)
    return jnp.sum(jnp.where(eye, jnp.broadcast_to(row, shape), 0.0), axis=1, keepdims=True)


def unpad(ref):
    return ref[...].reshape(C, PITCH, C)[:, :BLK].astype(BF16)


def project_block(load, block, mask, gain, bias, w, g, x_ref, gate_ref, sl_ref, sr_ref):
    for t in range(0, BLK, 2):
        s = block * BLK + t
        lines = jnp.concatenate([load(s), load(s + H), load(s + 1), load(s + 1 + H)], axis=0)
        normed = layer_norm(lines, gain, bias).astype(BF16)
        p = lax.dot_general(
            w, normed, (((0,), (1,)), ((), ())), preferred_element_type=F32
        )
        gate = sigmoid(jnp.dot(normed, g, preferred_element_type=F32))
        gate_ref[s] = gate[:C]
        gate_ref[s + 1] = gate[C:]
        left = sigmoid(p[:C]) * p[C : 2 * C]
        right = sigmoid(p[2 * C : 3 * C]) * p[3 * C :]
        for u in range(2):
            keep = mask(s + u)
            sl_ref[pl.ds(t + u, C, stride=PITCH), :] = left[:, u * C : (u + 1) * C] * keep
            sr_ref[pl.ds(t + u, C, stride=PITCH), :] = right[:, u * C : (u + 1) * C] * keep
    x_ref[:, pl.ds(pl.multiple_of(block * BLK, BLK), BLK), :] = unpad(sl_ref)
    x_ref[:, pl.ds(pl.multiple_of(H + block * BLK, BLK), BLK), :] = unpad(sr_ref)


def first_kernel(
    z_hbm, token_hbm, mask_hbm, gain_hbm, bias_hbm, w_hbm, g_hbm, x_hbm, gate_hbm, sl_ref, sr_ref,
    z_ref, token_ref, mask_ref, gain_ref, bias_ref, w_ref, g_ref, x_ref, gate_ref, small_sem, z_sem, out_sem,
):
    small = [
        pltpu.make_async_copy(source, to, small_sem.at[n])
        for n, (source, to) in enumerate(
            (
                (gain_hbm, gain_ref), (bias_hbm, bias_ref), (mask_hbm, mask_ref), (token_hbm, token_ref),
                (w_hbm.at[0], w_ref), (g_hbm.at[0], g_ref),
            )
        )
    ]
    parts = []
    for block in range(H // BLK):
        for half in range(2):
            lines = pl.ds(half * H + block * BLK, BLK)
            parts.append(pltpu.make_async_copy(z_hbm.at[lines], z_ref.at[lines], z_sem.at[len(parts)]))
    for copy in small + parts:
        copy.start()
    for copy in small:
        copy.wait()
    gain, bias = gain_ref[0:1], bias_ref[0:1]
    across = lanes_twice(mask_ref, col_block())
    start = row_block() * T
    copies = []
    for block in range(H // BLK):
        parts[2 * block].wait()
        parts[2 * block + 1].wait()
        project_block(
            lambda s: z_ref[s], block, lambda s: line_mask(token_ref, start, s, across), gain, bias,
            w_ref[...], g_ref[...], x_ref, gate_ref, sl_ref, sr_ref,
        )
        for half in range(2):
            lines = pl.ds(half * H + block * BLK, BLK)
            copies.append(
                pltpu.make_async_copy(x_ref.at[:, lines], x_hbm.at[:, lines], out_sem.at[len(copies)])
            )
            copies[-1].start()
        lines = pl.ds(block * BLK, BLK)
        copies.append(pltpu.make_async_copy(gate_ref.at[lines], gate_hbm.at[lines], out_sem.at[len(copies)]))
        copies[-1].start()
    for copy in copies:
        copy.wait()


def update_block(block, y_ref, gain, bias, ow, gate_ref, s_ref, emit):
    y = y_ref[:, pl.ds(pl.multiple_of(block * BLK, BLK), BLK), :].astype(F32)
    average = jnp.sum(y, axis=0) * (1.0 / C)
    centred = y - average[None]
    spread = jnp.sum(centred * centred, axis=0) * (1.0 / C)
    s_ref[: C * BLK] = (centred * lax.rsqrt(spread + 1e-05)[None]).reshape(C * BLK, C)
    for t in range(BLK):
        s = block * BLK + t
        normed = (s_ref[pl.ds(t, C, stride=BLK), :] * gain + bias).astype(BF16)
        update = lax.dot_general(
            normed, ow, (((0,), (0,)), ((), ())), preferred_element_type=F32
        )
        emit(s, gate_ref[s] * update)


def middle_kernel(
    y_ref, z_ref, gate0_ref, mgain_ref, mbias_ref, ow_ref, token_ref, mask_ref, gain_ref, bias_ref,
    w_ref, g_ref, x_ref, gate_ref, zn_ref, sl_ref, sr_ref, zp_ref,
):
    mgain, mbias = column(mgain_ref[0:1]), column(mbias_ref[0:1])
    gain, bias = gain_ref[1:2], bias_ref[1:2]
    across = lanes_twice(mask_ref, row_block())
    start = col_block() * T

    def emit(s, change):
        for i, part in ((s, change[:T]), (s + H, change[T:])):
            value = z_ref[i] + part
            zn_ref[i] = value
            zp_ref[pl.ds(pl.multiple_of(i * WIDE, 8), T), :] = value

    def body(block, carry):
        update_block(block, y_ref, mgain, mbias, ow_ref[0], gate0_ref, sl_ref, emit)
        return carry

    lax.fori_loop(0, H // BLK, body, 0)

    for block in range(H // BLK):
        project_block(
            lambda s: zp_ref[pl.ds(s, T, stride=WIDE), :], block, lambda s: line_mask(token_ref, start, s, across), gain, bias,
            w_ref[1], g_ref[1], x_ref, gate_ref, sl_ref, sr_ref,
        )


def last_kernel(y_ref, z_ref, gate_ref, mgain_ref, mbias_ref, ow_ref, out_hbm, s_ref, c_ref, out_ref, sem):
    mgain, mbias = column(mgain_ref[1:2]), column(mbias_ref[1:2])

    def emit(s, change):
        c_ref[pl.ds(s, T, stride=WIDE), :] = change[:T]
        c_ref[pl.ds(s + H, T, stride=WIDE), :] = change[T:]

    for block in range(H // BLK):
        update_block(block, y_ref, mgain, mbias, ow_ref[1], gate_ref, s_ref, emit)
    copies = []
    for part in range(4):
        for i in range(part * 16, (part + 1) * 16):
            out_ref[i] = z_ref[i] + c_ref[i * WIDE : i * WIDE + T]
        lines = pl.ds(part * 16, 16)
        copies.append(pltpu.make_async_copy(out_ref.at[lines], out_hbm.at[lines], sem.at[part]))
        copies[-1].start()
    for copy in copies:
        copy.wait()


def sides(x0, x1):
    low = jnp.concatenate([x0[:, :T], x1[:, :T]], axis=1)
    high = jnp.concatenate([x0[:, T:], x1[:, T:]], axis=1)
    return low, high


def nt_dot(a, b):
    return lax.dot_general(a, b, (((1,), (1,)), ((), ())), preferred_element_type=F32)


def chip(row, col):
    return lax.div(row, 2) * 16 + lax.rem(col, 2) * 8 + lax.rem(row, 2) * 4 + lax.div(col, 2)


def outgoing_kernel(x_ref, l_ref, r_ref, other_ref, rs_ref):
    core = lax.axis_index("core")

    def gather(row, carry):
        at = pl.multiple_of(row * T, T)
        to = pl.multiple_of(lax.rem(row, 2) * 512 + lax.div(row, 2) * T, T)
        base = chip(row, 0)
        for q in range(4):
            low, high = sides(x_ref[base + q], x_ref[base + 8 + q])
            cols = slice(q * 128, (q + 1) * 128)
            l_ref[pl.ds(at, H), cols] = low[:H]
            l_ref[pl.ds(at + H, H), cols] = high[:H]
            rs_ref[pl.ds(to, H), cols] = low[H:]
            rs_ref[pl.ds(to + H, H), cols] = high[H:]
        return carry

    lax.fori_loop(0, 16, gather, 0)
    r_ref[...] = rs_ref[pl.ds(pl.multiple_of(core * 512, 512), 512), :]
    send = rs_ref[pl.ds(pl.multiple_of((1 - core) * 512, 512), 512), :]

    def multiply(i, carry):
        rows = pl.ds(pl.multiple_of(i * 256, 256), 256)
        other_ref[rows, :] = nt_dot(l_ref[rows, :], send).astype(BF16)
        return carry

    lax.fori_loop(0, 4, multiply, 0)


def outgoing_sum_kernel(l_ref, r_ref, got_ref, y_ref):
    def body(i, carry):
        rows = pl.ds(pl.multiple_of(i * 256, 256), 256)
        total = (nt_dot(l_ref[rows, :], r_ref[...]) + got_ref[rows, :].astype(F32)).astype(BF16)
        for b in range(4):
            base = chip(i * 4 + b, 0)
            for q in range(4):
                part = total[b * T : (b + 1) * T, q * 128 : (q + 1) * 128]
                first, second = sides(part[:H], part[H:])
                y_ref[base + q] = first
                y_ref[base + 8 + q] = second
        return carry

    lax.fori_loop(0, 4, body, 0)


def incoming_kernel(x_ref, l_ref, r_ref):
    def gather(c, carry):
        at = pl.multiple_of(c * T, T)
        base = chip(0, c)
        for q in range(8):
            low, high = sides(x_ref[16 * q + base], x_ref[16 * q + 4 + base])
            cols = slice(q * 128, (q + 1) * 128)
            l_ref[pl.ds(at, H), cols] = low[:H]
            l_ref[pl.ds(at + H, H), cols] = high[:H]
            r_ref[pl.ds(at, H), cols] = low[H:]
            r_ref[pl.ds(at + H, H), cols] = high[H:]
        return carry

    lax.fori_loop(0, 8, gather, 0)


def incoming_half(l_ref, r_ref, write):
    def body(i, carry):
        right = r_ref[pl.ds(pl.multiple_of(i * 128, 128), 128), :]
        total = nt_dot(right, l_ref[...]).astype(BF16)
        for b in range(2):
            base = chip(0, i * 2 + b)
            for q in range(4):
                part = total[b * T : (b + 1) * T, q * 128 : (q + 1) * 128]
                first, second = sides(part[:H], part[H:])
                write(2 * q, base, first)
                write(2 * q + 1, base, second)
        return carry

    lax.fori_loop(0, 4, body, 0)


def incoming_own_kernel(l_ref, r_ref, half_ref):
    def write(plane, base, value):
        half_ref[plane * 16 + base] = value

    incoming_half(l_ref, r_ref, write)


def incoming_sum_kernel(l_ref, r_ref, half_ref, y_ref):
    own = lax.axis_index("core")

    def write(plane, base, value):
        y_ref[plane * 16 + (1 - own) * 4 + base] = value

    incoming_half(l_ref, r_ref, write)
    for plane in range(8):
        for y in range(2):
            y_ref[pl.ds(plane * 16 + y * 8 + own * 4, 4)] = half_ref[pl.ds(plane * 16 + y * 8, 4)]


def call(kernel, outs, scratch=(), specs=None, out_specs=None, limit=VMEM_LIMIT):
    return pl.pallas_call(
        kernel,
        out_shape=[jax.ShapeDtypeStruct(s, d) for s, d in outs],
        scratch_shapes=[pltpu.VMEM(*m) if isinstance(m, tuple) else m for m in scratch],
        compiler_params=pltpu.CompilerParams(vmem_limit_bytes=limit),
        **({} if specs is None else {"in_specs": specs}),
        **({} if out_specs is None else {"out_specs": out_specs}),
    )


VMEM_SPEC = pl.BlockSpec(memory_space=pltpu.VMEM)
SMEM_SPEC = pl.BlockSpec(memory_space=pltpu.SMEM)
HBM_SPEC = pl.BlockSpec(memory_space=pltpu.HBM)
CHIPS = ("z", "yh", "yl", "x")
SWAP = ((0, 1), (1, 0))


def exchange(x):
    return lax.all_to_all(x, CHIPS, split_axis=0, concat_axis=0, tiled=True)


def on_device(
    pair, token_mask, in_gain, in_bias, proj_weight, gate_weight, mid_gain, mid_bias, out_weight
):
    mask = token_mask[None]
    gates = ((H, 2 * T, C), F32)
    wide = ((C, T, 2 * T), BF16)
    narrow = ((C, H, 2 * T), BF16)
    line = ((C * PITCH, 2 * T), F32)
    tile = ((T * WIDE, C), F32)

    x, gate0 = call(
        first_kernel,
        [wide, gates],
        [
            line, line, ((T, T, C), F32), pltpu.SMEM((1024,), jnp.int32), ((1, 1024), jnp.int32), ((2, C), F32),
            ((2, C), F32), ((C, 4 * C), BF16), ((C, C), BF16), wide, gates, pltpu.SemaphoreType.DMA((6,)),
            pltpu.SemaphoreType.DMA((4,)), pltpu.SemaphoreType.DMA((6,)),
        ],
        [HBM_SPEC] * 7,
        [HBM_SPEC] * 2,
        FIRST_LIMIT,
    )(
        pair, token_mask, mask, in_gain, in_bias, proj_weight, gate_weight
    )
    x = exchange(x)
    left, right, other = call(
        outgoing_kernel,
        [((1024, 512), BF16), ((512, 512), BF16), ((1024, 512), BF16)],
        [((1024, 512), BF16)],
    )(x)
    got = lax.ppermute(other, "core", SWAP)
    (y,) = call(outgoing_sum_kernel, [narrow])(left, right, got)
    y = exchange(y)
    x, gate1, current = call(middle_kernel, [wide, gates, ((T, T, C), F32)], [line, line, tile], [VMEM_SPEC] * 6 + [SMEM_SPEC] + [VMEM_SPEC] * 5)(
        y, pair, gate0, mid_gain, mid_bias, out_weight,
        token_mask, mask, in_gain, in_bias, proj_weight, gate_weight,
    )
    x = exchange(x)
    left, right = call(incoming_kernel, [((512, 1024), BF16), ((512, 1024), BF16)])(x)
    got = lax.ppermute(left, "core", SWAP)
    (half,) = call(incoming_own_kernel, [narrow])(left, right)
    (y,) = call(incoming_sum_kernel, [narrow])(got, right, half)
    y = exchange(y)
    (out,) = call(
        last_kernel,
        [((T, T, C), F32)],
        [line, tile, ((T, T, C), F32), pltpu.SemaphoreType.DMA((4,))],
        [VMEM_SPEC] * 6,
        [HBM_SPEC],
    )(
        y, current, gate1, mid_gain, mid_bias, out_weight
    )
    return out


def solution(mesh):
    inner = jax.sharding.Mesh(mesh.devices.reshape(8, 2, 4, 2, 2), ("z", "yl", "x", "yh", "core"))
    spec = P(("z", "yl"), ("x", "yh", "core"), None)
    return jax.shard_map(
        on_device,
        mesh=inner,
        in_specs=(spec, P(), P(), P(), P(), P(), P(), P(), P()),
        out_specs=spec,
        check_vma=False,
    )
```

```python
import jax
import jax.numpy as jnp
from jax import lax
from jax.experimental import pallas as pl
from jax.experimental.pallas import tpu as pltpu
from jax.sharding import PartitionSpec as P

F32 = jnp.float32
BF16 = jnp.bfloat16
C = 128
T = 64
H = 32
PITCH = 24
WIDE = 72
BLK = 16
VMEM_LIMIT = 24 * 1024 * 1024
FIRST_LIMIT = 56 * 1024 * 1024


def sigmoid(x):
    return 0.5 * jnp.tanh(0.5 * x) + 0.5


def layer_norm(values, gain, bias):
    average = jnp.mean(values, axis=-1, keepdims=True)
    centred = values - average
    spread = jnp.mean(centred * centred, axis=-1, keepdims=True)
    return centred * lax.rsqrt(spread + 1e-05) * gain + bias


def lanes_twice(mask_ref, block):
    chunk = mask_ref[:, pl.ds(pl.multiple_of(lax.div(block, 2) * 2 * T, 2 * T), 2 * T)].astype(F32)
    turned = jnp.concatenate([chunk[:, T:], chunk[:, :T]], axis=1)
    lane = lax.broadcasted_iota(jnp.int32, (1, 2 * T), 1)
    keep = lax.div(lane, T) == lax.rem(block, 2)
    return jnp.where(keep, chunk, turned)


def line_mask(token_ref, start, s, across):
    lane = lax.broadcasted_iota(jnp.int32, (1, 2 * T), 1)
    first, second = token_ref[start + s].astype(F32), token_ref[start + s + H].astype(F32)
    return jnp.where(lane < T, first, second) * across


def row_block():
    return lax.axis_index("z") * 2 + lax.axis_index("yl")


def col_block():
    return lax.axis_index("x") * 4 + lax.axis_index("yh") * 2 + lax.axis_index("core")


def column(row):
    shape = (C, C)
    eye = lax.broadcasted_iota(jnp.int32, shape, 0) == lax.broadcasted_iota(jnp.int32, shape, 1)
    return jnp.sum(jnp.where(eye, jnp.broadcast_to(row, shape), 0.0), axis=1, keepdims=True)


def unpad(ref):
    return ref[...].reshape(C, PITCH, C)[:, :BLK].astype(BF16)


def project_block(load, block, mask, gain, bias, w, g, x_ref, gate_ref, sl_ref, sr_ref):
    for t in range(0, BLK, 2):
        s = block * BLK + t
        lines = jnp.concatenate([load(s), load(s + H), load(s + 1), load(s + 1 + H)], axis=0)
        normed = layer_norm(lines, gain, bias).astype(BF16)
        p = lax.dot_general(
            w, normed, (((0,), (1,)), ((), ())), preferred_element_type=F32
        )
        gate = sigmoid(jnp.dot(normed, g, preferred_element_type=F32))
        gate_ref[s] = gate[:C]
        gate_ref[s + 1] = gate[C:]
        left = sigmoid(p[:C]) * p[C : 2 * C]
        right = sigmoid(p[2 * C : 3 * C]) * p[3 * C :]
        for u in range(2):
            keep = mask(s + u)
            sl_ref[pl.ds(t + u, C, stride=PITCH), :] = left[:, u * C : (u + 1) * C] * keep
            sr_ref[pl.ds(t + u, C, stride=PITCH), :] = right[:, u * C : (u + 1) * C] * keep
    x_ref[:, pl.ds(pl.multiple_of(block * BLK, BLK), BLK), :] = unpad(sl_ref)
    x_ref[:, pl.ds(pl.multiple_of(H + block * BLK, BLK), BLK), :] = unpad(sr_ref)


def first_kernel(
    z_hbm, token_hbm, mask_hbm, gain_hbm, bias_hbm, w_hbm, g_hbm, x_hbm, gate_hbm, sl_ref, sr_ref,
    z_ref, token_ref, mask_ref, gain_ref, bias_ref, w_ref, g_ref, x_ref, gate_ref, small_sem, z_sem, out_sem,
):
    small = [
        pltpu.make_async_copy(source, to, small_sem.at[n])
        for n, (source, to) in enumerate(
            (
                (gain_hbm, gain_ref), (bias_hbm, bias_ref), (mask_hbm, mask_ref), (token_hbm, token_ref),
                (w_hbm.at[0], w_ref), (g_hbm.at[0], g_ref),
            )
        )
    ]
    parts = []
    for block in range(H // BLK):
        for half in range(2):
            lines = pl.ds(half * H + block * BLK, BLK)
            parts.append(pltpu.make_async_copy(z_hbm.at[lines], z_ref.at[lines], z_sem.at[len(parts)]))
    for copy in small + parts:
        copy.start()
    for copy in small:
        copy.wait()
    gain, bias = gain_ref[0:1], bias_ref[0:1]
    across = lanes_twice(mask_ref, col_block())
    start = row_block() * T
    copies = []
    for block in range(H // BLK):
        parts[2 * block].wait()
        parts[2 * block + 1].wait()
        project_block(
            lambda s: z_ref[s], block, lambda s: line_mask(token_ref, start, s, across), gain, bias,
            w_ref[...], g_ref[...], x_ref, gate_ref, sl_ref, sr_ref,
        )
        for half in range(2):
            lines = pl.ds(half * H + block * BLK, BLK)
            copies.append(
                pltpu.make_async_copy(x_ref.at[:, lines], x_hbm.at[:, lines], out_sem.at[len(copies)])
            )
            copies[-1].start()
        lines = pl.ds(block * BLK, BLK)
        copies.append(pltpu.make_async_copy(gate_ref.at[lines], gate_hbm.at[lines], out_sem.at[len(copies)]))
        copies[-1].start()
    for copy in copies:
        copy.wait()


def update_block(block, y_ref, gain, bias, ow, gate_ref, s_ref, emit):
    y = y_ref[:, pl.ds(pl.multiple_of(block * BLK, BLK), BLK), :].astype(F32)
    average = jnp.sum(y, axis=0) * (1.0 / C)
    centred = y - average[None]
    spread = jnp.sum(centred * centred, axis=0) * (1.0 / C)
    s_ref[: C * BLK] = (centred * lax.rsqrt(spread + 1e-05)[None]).reshape(C * BLK, C)
    for t in range(0, BLK, 4):
        lines = jnp.concatenate([s_ref[pl.ds(t + u, C, stride=BLK), :] for u in range(4)], axis=1)
        normed = (lines * gain + bias).astype(BF16)
        update = lax.dot_general(normed, ow, (((0,), (0,)), ((), ())), preferred_element_type=F32)
        for u in range(4):
            s = block * BLK + t + u
            emit(s, gate_ref[s] * update[u * C : (u + 1) * C])


def middle_kernel(
    y_ref, z_ref, gate0_ref, mgain_ref, mbias_ref, ow_ref, token_ref, mask_ref, gain_ref, bias_ref,
    w_ref, g_ref, x_ref, gate_ref, zn_ref, sl_ref, sr_ref, zp_ref,
):
    mgain, mbias = column(mgain_ref[0:1]), column(mbias_ref[0:1])
    gain, bias = gain_ref[1:2], bias_ref[1:2]
    across = lanes_twice(mask_ref, row_block())
    start = col_block() * T

    def emit(s, change):
        for i, part in ((s, change[:T]), (s + H, change[T:])):
            value = z_ref[i] + part
            zn_ref[i] = value
            zp_ref[pl.ds(pl.multiple_of(i * WIDE, 8), T), :] = value

    for block in range(H // BLK):
        update_block(block, y_ref, mgain, mbias, ow_ref[0], gate0_ref, sl_ref, emit)
    for block in range(H // BLK):
        project_block(
            lambda s: zp_ref[pl.ds(s, T, stride=WIDE), :], block, lambda s: line_mask(token_ref, start, s, across), gain, bias,
            w_ref[1], g_ref[1], x_ref, gate_ref, sl_ref, sr_ref,
        )


def last_kernel(y_ref, z_ref, gate_ref, mgain_ref, mbias_ref, ow_ref, out_hbm, s_ref, c_ref, out_ref, sem):
    mgain, mbias = column(mgain_ref[1:2]), column(mbias_ref[1:2])

    def emit(s, change):
        c_ref[pl.ds(s, T, stride=WIDE), :] = change[:T]
        c_ref[pl.ds(s + H, T, stride=WIDE), :] = change[T:]

    for block in range(H // BLK):
        update_block(block, y_ref, mgain, mbias, ow_ref[1], gate_ref, s_ref, emit)
    copies = []
    for part in range(4):
        for i in range(part * 16, (part + 1) * 16):
            out_ref[i] = z_ref[i] + c_ref[i * WIDE : i * WIDE + T]
        lines = pl.ds(part * 16, 16)
        copies.append(pltpu.make_async_copy(out_ref.at[lines], out_hbm.at[lines], sem.at[part]))
        copies[-1].start()
    for copy in copies:
        copy.wait()


def sides(x0, x1):
    low = jnp.concatenate([x0[:, :T], x1[:, :T]], axis=1)
    high = jnp.concatenate([x0[:, T:], x1[:, T:]], axis=1)
    return low, high


def nt_dot(a, b):
    return lax.dot_general(a, b, (((1,), (1,)), ((), ())), preferred_element_type=F32)


def chip(row, col):
    return lax.div(row, 2) * 16 + lax.rem(col, 2) * 8 + lax.rem(row, 2) * 4 + lax.div(col, 2)


def spread_rows(to_ref, at, cols, x0, x1):
    low, high = sides(x0, x1)
    to_ref[pl.ds(at, H), cols] = low
    to_ref[pl.ds(at + H, H), cols] = high


def gather_right(x_ref, parity, to_ref):
    for m in range(8):
        for q in range(4):
            base = m * 16 + parity * 4 + q
            spread_rows(to_ref, m * T, slice(q * 128, (q + 1) * 128), x_ref[base, H:], x_ref[base + 8, H:])


def outgoing_other_kernel(x_ref, l_ref, other_ref, rs_ref):
    gather_right(x_ref, 1 - lax.axis_index("core"), rs_ref)
    for row in range(16):
        for q in range(4):
            base = (row // 2) * 16 + (row % 2) * 4 + q
            spread_rows(l_ref, row * T, slice(q * 128, (q + 1) * 128), x_ref[base, :H], x_ref[base + 8, :H])
    for i in range(2):
        rows = slice(i * 512, (i + 1) * 512)
        other_ref[rows, :] = nt_dot(l_ref[rows, :], rs_ref[...]).astype(BF16)


def outgoing_own_kernel(x_ref, l_ref, own_ref, rs_ref):
    gather_right(x_ref, lax.axis_index("core"), rs_ref)
    for i in range(2):
        rows = slice(i * 512, (i + 1) * 512)
        own_ref[rows, :] = nt_dot(l_ref[rows, :], rs_ref[...])


def outgoing_sum_kernel(own_ref, got_ref, y_ref):
    for row in range(16):
        rows = slice(row * T, (row + 1) * T)
        total = (own_ref[rows, :] + got_ref[rows, :].astype(F32)).astype(BF16)
        base = (row // 2) * 16 + (row % 2) * 4
        for q in range(4):
            part = total[:, q * 128 : (q + 1) * 128]
            first, second = sides(part[:H], part[H:])
            y_ref[base + q] = first
            y_ref[base + 8 + q] = second


def incoming_left_kernel(x_ref, l_ref):
    for c in range(8):
        base = (c % 2) * 8 + c // 2
        for q in range(8):
            cols = slice(q * 128, (q + 1) * 128)
            spread_rows(l_ref, c * T, cols, x_ref[16 * q + base, :H], x_ref[16 * q + 4 + base, :H])


def incoming_half(l_ref, r_ref, write):
    total = nt_dot(r_ref[...], l_ref[...]).astype(BF16)
    for c in range(8):
        base = (c % 2) * 8 + c // 2
        for q in range(4):
            part = total[c * T : (c + 1) * T, q * 128 : (q + 1) * 128]
            first, second = sides(part[:H], part[H:])
            write(2 * q, base, first)
            write(2 * q + 1, base, second)


def incoming_own_kernel(x_ref, l_ref, r_ref, half_ref):
    for c in range(8):
        base = (c % 2) * 8 + c // 2
        for q in range(8):
            cols = slice(q * 128, (q + 1) * 128)
            spread_rows(r_ref, c * T, cols, x_ref[16 * q + base, H:], x_ref[16 * q + 4 + base, H:])

    def write(plane, base, value):
        half_ref[plane * 8 + base // 8 * 4 + base % 4] = value

    incoming_half(l_ref, r_ref, write)


def incoming_sum_kernel(l_ref, r_ref, half_ref, y_ref):
    own = lax.axis_index("core")

    def write(plane, base, value):
        y_ref[plane * 16 + (1 - own) * 4 + base] = value

    incoming_half(l_ref, r_ref, write)
    for plane in range(8):
        for y in range(2):
            y_ref[pl.ds(plane * 16 + y * 8 + own * 4, 4)] = half_ref[plane * 8 + y * 4 : plane * 8 + y * 4 + 4]


def call(kernel, outs, scratch=(), specs=None, out_specs=None, limit=VMEM_LIMIT):
    return pl.pallas_call(
        kernel,
        out_shape=[jax.ShapeDtypeStruct(s, d) for s, d in outs],
        scratch_shapes=[pltpu.VMEM(*m) if isinstance(m, tuple) else m for m in scratch],
        compiler_params=pltpu.CompilerParams(vmem_limit_bytes=limit),
        **({} if specs is None else {"in_specs": specs}),
        **({} if out_specs is None else {"out_specs": out_specs}),
    )


VMEM_SPEC = pl.BlockSpec(memory_space=pltpu.VMEM)
SMEM_SPEC = pl.BlockSpec(memory_space=pltpu.SMEM)
HBM_SPEC = pl.BlockSpec(memory_space=pltpu.HBM)
CHIPS = ("z", "yh", "yl", "x")
SWAP = ((0, 1), (1, 0))


def exchange(x):
    return lax.all_to_all(x, CHIPS, split_axis=0, concat_axis=0, tiled=True)


def on_device(
    pair, token_mask, in_gain, in_bias, proj_weight, gate_weight, mid_gain, mid_bias, out_weight
):
    mask = token_mask[None]
    gates = ((H, 2 * T, C), F32)
    wide = ((C, T, 2 * T), BF16)
    narrow = ((C, H, 2 * T), BF16)
    line = ((C * PITCH, 2 * T), F32)
    tile = ((T * WIDE, C), F32)

    x, gate0 = call(
        first_kernel,
        [wide, gates],
        [
            line, line, ((T, T, C), F32), pltpu.SMEM((1024,), jnp.int32), ((1, 1024), jnp.int32), ((2, C), F32),
            ((2, C), F32), ((C, 4 * C), BF16), ((C, C), BF16), wide, gates, pltpu.SemaphoreType.DMA((6,)),
            pltpu.SemaphoreType.DMA((4,)), pltpu.SemaphoreType.DMA((6,)),
        ],
        [HBM_SPEC] * 7,
        [HBM_SPEC] * 2,
        FIRST_LIMIT,
    )(
        pair, token_mask, mask, in_gain, in_bias, proj_weight, gate_weight
    )
    x = exchange(x)
    right = ((512, 512), BF16)
    left, other = call(outgoing_other_kernel, [((1024, 512), BF16), ((1024, 512), BF16)], [right])(x)
    got = lax.ppermute(other, "core", SWAP)
    (own,) = call(outgoing_own_kernel, [((1024, 512), F32)], [right])(x, left)
    (y,) = call(outgoing_sum_kernel, [narrow])(own, got)
    y = exchange(y)
    x, gate1, current = call(middle_kernel, [wide, gates, ((T, T, C), F32)], [line, line, tile], [VMEM_SPEC] * 6 + [SMEM_SPEC] + [VMEM_SPEC] * 5)(
        y, pair, gate0, mid_gain, mid_bias, out_weight,
        token_mask, mask, in_gain, in_bias, proj_weight, gate_weight,
    )
    x = exchange(x)
    side = ((512, 1024), BF16)
    (left,) = call(incoming_left_kernel, [side])(x)
    got = lax.ppermute(left, "core", SWAP)
    right, half = call(incoming_own_kernel, [side, ((64, H, 2 * T), BF16)])(x, left)
    (y,) = call(incoming_sum_kernel, [narrow])(got, right, half)
    y = exchange(y)
    (out,) = call(
        last_kernel,
        [((T, T, C), F32)],
        [line, tile, ((T, T, C), F32), pltpu.SemaphoreType.DMA((4,))],
        [VMEM_SPEC] * 6,
        [HBM_SPEC],
    )(
        y, current, gate1, mid_gain, mid_bias, out_weight
    )
    return out


def solution(mesh):
    inner = jax.sharding.Mesh(mesh.devices.reshape(8, 2, 4, 2, 2), ("z", "yl", "x", "yh", "core"))
    spec = P(("z", "yl"), ("x", "yh", "core"), None)
    return jax.shard_map(
        on_device,
        mesh=inner,
        in_specs=(spec, P(), P(), P(), P(), P(), P(), P(), P()),
        out_specs=spec,
        check_vma=False,
    )
```

```python
import jax
import jax.numpy as jnp
from jax import lax
from jax.experimental import pallas as pl
from jax.experimental.pallas import tpu as pltpu
from jax.sharding import PartitionSpec as P

F32 = jnp.float32
BF16 = jnp.bfloat16
C = 128
T = 64
H = 32
PITCH = 24
WIDE = 72
BLK = 16
VMEM_LIMIT = 24 * 1024 * 1024
FIRST_LIMIT = 56 * 1024 * 1024


def halved(weights):
    return (weights.astype(F32) * 0.5).astype(BF16)


def gate_weights_halved(w):
    blocks = [w[:, i * C : (i + 1) * C] for i in range(4)]
    return jnp.concatenate([halved(blocks[0]), blocks[1], halved(blocks[2]), blocks[3]], axis=1)


def layer_norm(values, gain, bias):
    average = jnp.mean(values, axis=-1, keepdims=True)
    centred = values - average
    spread = jnp.mean(centred * centred, axis=-1, keepdims=True)
    return centred * lax.rsqrt(spread + 1e-05) * gain + bias


def lanes_twice(mask_ref, block):
    chunk = mask_ref[:, pl.ds(pl.multiple_of(lax.div(block, 2) * 2 * T, 2 * T), 2 * T)].astype(F32)
    turned = jnp.concatenate([chunk[:, T:], chunk[:, :T]], axis=1)
    lane = lax.broadcasted_iota(jnp.int32, (1, 2 * T), 1)
    keep = lax.div(lane, T) == lax.rem(block, 2)
    return jnp.where(keep, chunk, turned) * 0.5


def line_mask(token_ref, start, s, across):
    lane = lax.broadcasted_iota(jnp.int32, (1, 2 * T), 1)
    first, second = token_ref[start + s].astype(F32), token_ref[start + s + H].astype(F32)
    return jnp.where(lane < T, first, second) * across


def row_block():
    return lax.axis_index("z") * 2 + lax.axis_index("yl")


def col_block():
    return lax.axis_index("x") * 4 + lax.axis_index("yh") * 2 + lax.axis_index("core")


def column(row):
    shape = (C, C)
    eye = lax.broadcasted_iota(jnp.int32, shape, 0) == lax.broadcasted_iota(jnp.int32, shape, 1)
    return jnp.sum(jnp.where(eye, jnp.broadcast_to(row, shape), 0.0), axis=1, keepdims=True)


def unpad(ref):
    return ref[: C * PITCH].reshape(C, PITCH, C)[:, :BLK].astype(BF16)


def project_block(load, block, mask, gain, bias, w, g, x_ref, keep_gate, sl_ref, sr_ref):
    for t in range(0, BLK, 2):
        s = block * BLK + t
        lines = jnp.concatenate([load(s), load(s + H), load(s + 1), load(s + 1 + H)], axis=0)
        normed = layer_norm(lines, gain, bias).astype(BF16)
        p = lax.dot_general(
            w, normed, (((0,), (1,)), ((), ())), preferred_element_type=F32
        )
        gate = jnp.tanh(jnp.dot(normed, g, preferred_element_type=F32)) + 1.0
        keep_gate(s, gate[:C])
        keep_gate(s + 1, gate[C:])
        left = (jnp.tanh(p[:C]) + 1.0) * p[C : 2 * C]
        right = (jnp.tanh(p[2 * C : 3 * C]) + 1.0) * p[3 * C :]
        for u in range(2):
            keep = mask(s + u)
            sl_ref[pl.ds(t + u, C, stride=PITCH), :] = left[:, u * C : (u + 1) * C] * keep
            sr_ref[pl.ds(t + u, C, stride=PITCH), :] = right[:, u * C : (u + 1) * C] * keep
    x_ref[:, pl.ds(pl.multiple_of(block * BLK, BLK), BLK), :] = unpad(sl_ref)
    x_ref[:, pl.ds(pl.multiple_of(H + block * BLK, BLK), BLK), :] = unpad(sr_ref)


def first_kernel(
    z_hbm, token_hbm, mask_hbm, gain_hbm, bias_hbm, w_hbm, g_hbm, x_hbm, gate_hbm, sl_ref, sr_ref,
    z_ref, token_ref, mask_ref, gain_ref, bias_ref, w_ref, g_ref, x_ref, gate_ref, small_sem, z_sem, out_sem,
):
    small = [
        pltpu.make_async_copy(source, to, small_sem.at[n])
        for n, (source, to) in enumerate(
            (
                (gain_hbm, gain_ref), (bias_hbm, bias_ref), (mask_hbm, mask_ref), (token_hbm, token_ref),
                (w_hbm.at[0], w_ref), (g_hbm.at[0], g_ref),
            )
        )
    ]
    parts = []
    for n in range(T // BLK):
        lines = pl.ds(n % 2 * H + n // 2 * BLK, BLK)
        parts.append(pltpu.make_async_copy(z_hbm.at[lines], z_ref.at[lines], z_sem.at[n]))
    for copy in parts[:2] + small + parts[2:]:
        copy.start()
    for copy in small:
        copy.wait()
    gain, bias = gain_ref[0:1], bias_ref[0:1]
    across = lanes_twice(mask_ref, col_block())
    start = row_block() * T
    w, g = gate_weights_halved(w_ref[...]), halved(g_ref[...])
    copies = []

    def keep_gate(s, value):
        gate_ref[s] = value

    def send(source, to):
        copies.append(pltpu.make_async_copy(source, to, out_sem.at[len(copies)]))
        copies[-1].start()

    for block in range(H // BLK):
        parts[2 * block].wait()
        parts[2 * block + 1].wait()
        project_block(
            lambda s: z_ref[s], block, lambda s: line_mask(token_ref, start, s, across), gain, bias,
            w, g, x_ref, keep_gate, sl_ref, sr_ref,
        )
        for half in range(2):
            lines = pl.ds(half * H + block * BLK, BLK)
            send(x_ref.at[:, lines], x_hbm.at[:, lines])
        lines = pl.ds(block * BLK, BLK)
        send(gate_ref.at[lines], gate_hbm.at[lines])
    for copy in copies:
        copy.wait()


def update_block(block, y_ref, gain, bias, ow, s_ref, emit):
    y = y_ref[:, pl.ds(pl.multiple_of(block * BLK, BLK), BLK), :].astype(F32)
    average = jnp.sum(y, axis=0) * (1.0 / C)
    centred = y - average[None]
    spread = jnp.sum(centred * centred, axis=0) * (1.0 / C)
    s_ref[: C * BLK] = (centred * lax.rsqrt(spread + 1e-05)[None]).reshape(C * BLK, C)
    for t in range(0, BLK, 4):
        lines = jnp.concatenate([s_ref[pl.ds(t + u, C, stride=BLK), :] for u in range(4)], axis=1)
        normed = (lines * gain + bias).astype(BF16)
        update = lax.dot_general(normed, ow, (((0,), (0,)), ((), ())), preferred_element_type=F32)
        for u in range(4):
            s = block * BLK + t + u
            emit(s, update[u * C : (u + 1) * C])


def middle_kernel(
    y_ref, z_ref, gate0_ref, mgain_ref, mbias_ref, ow_ref, token_ref, mask_ref, gain_ref, bias_ref,
    w_ref, g_ref, x_ref, gate_ref, zp_ref, sl_ref, sr_ref,
):
    mgain, mbias = column(mgain_ref[0:1]), column(mbias_ref[0:1])
    gain, bias = gain_ref[1:2], bias_ref[1:2]
    across = lanes_twice(mask_ref, row_block())
    start = col_block() * T
    w, g = gate_weights_halved(w_ref[1]), halved(g_ref[1])

    def keep_gate(s, value):
        gate_ref[pl.ds(s, T, stride=WIDE), :] = value[:T]
        gate_ref[pl.ds(s + H, T, stride=WIDE), :] = value[T:]

    def emit(s, update):
        change = gate0_ref[s] * update
        for i, part in ((s, change[:T]), (s + H, change[T:])):
            zp_ref[pl.ds(pl.multiple_of(i * WIDE, 8), T), :] = z_ref[i] + part

    for block in range(H // BLK):
        update_block(block, y_ref, mgain, mbias, halved(ow_ref[0]), sl_ref, emit)
    for block in range(H // BLK):
        project_block(
            lambda s: zp_ref[pl.ds(s, T, stride=WIDE), :], block, lambda s: line_mask(token_ref, start, s, across), gain, bias,
            w, g, x_ref, keep_gate, sl_ref, sr_ref,
        )


def last_kernel(y_ref, z_ref, gate_ref, mgain_ref, mbias_ref, ow_ref, out_hbm, s_ref, out_ref, sem):
    mgain, mbias = column(mgain_ref[1:2]), column(mbias_ref[1:2])

    def emit(s, update):
        for i, part in ((s, update[:T]), (s + H, update[T:])):
            rows = slice(i * WIDE, i * WIDE + T)
            out_ref[i] = z_ref[rows, :] + gate_ref[rows, :] * part

    copies = []
    for block in range(H // BLK):
        update_block(block, y_ref, mgain, mbias, halved(ow_ref[1]), s_ref, emit)
        for half in range(2):
            lines = pl.ds(half * H + block * BLK, BLK)
            copies.append(pltpu.make_async_copy(out_ref.at[lines], out_hbm.at[lines], sem.at[len(copies)]))
            copies[-1].start()
    for copy in copies:
        copy.wait()


def sides(x0, x1):
    low = jnp.concatenate([x0[:, :T], x1[:, :T]], axis=1)
    high = jnp.concatenate([x0[:, T:], x1[:, T:]], axis=1)
    return low, high


def nt_dot(a, b):
    return lax.dot_general(a, b, (((1,), (1,)), ((), ())), preferred_element_type=F32)


def chip(row, col):
    return lax.div(row, 2) * 16 + lax.rem(col, 2) * 8 + lax.rem(row, 2) * 4 + lax.div(col, 2)


def spread_rows(to_ref, at, cols, x0, x1):
    low, high = sides(x0, x1)
    to_ref[pl.ds(at, H), cols] = low
    to_ref[pl.ds(at + H, H), cols] = high


def gather_right(x_ref, parity, to_ref):
    for m in range(8):
        for q in range(4):
            base = m * 16 + parity * 4 + q
            spread_rows(to_ref, m * T, slice(q * 128, (q + 1) * 128), x_ref[base, H:], x_ref[base + 8, H:])


def outgoing_other_kernel(x_ref, l_ref, other_ref, rs_ref):
    gather_right(x_ref, 1 - lax.axis_index("core"), rs_ref)
    for row in range(16):
        for q in range(4):
            base = (row // 2) * 16 + (row % 2) * 4 + q
            spread_rows(l_ref, row * T, slice(q * 128, (q + 1) * 128), x_ref[base, :H], x_ref[base + 8, :H])
    for i in range(2):
        rows = slice(i * 512, (i + 1) * 512)
        other_ref[rows, :] = nt_dot(l_ref[rows, :], rs_ref[...]).astype(BF16)


def outgoing_own_kernel(x_ref, l_ref, own_ref, rs_ref):
    gather_right(x_ref, lax.axis_index("core"), rs_ref)
    for i in range(2):
        rows = slice(i * 512, (i + 1) * 512)
        own_ref[rows, :] = nt_dot(l_ref[rows, :], rs_ref[...])


def outgoing_sum_kernel(own_ref, got_ref, y_ref):
    for row in range(16):
        rows = slice(row * T, (row + 1) * T)
        total = (own_ref[rows, :] + got_ref[rows, :].astype(F32)).astype(BF16)
        base = (row // 2) * 16 + (row % 2) * 4
        for q in range(4):
            part = total[:, q * 128 : (q + 1) * 128]
            first, second = sides(part[:H], part[H:])
            y_ref[base + q] = first
            y_ref[base + 8 + q] = second


def incoming_left_kernel(x_ref, l_ref):
    for c in range(8):
        base = (c % 2) * 8 + c // 2
        for q in range(8):
            cols = slice(q * 128, (q + 1) * 128)
            spread_rows(l_ref, c * T, cols, x_ref[16 * q + base, :H], x_ref[16 * q + 4 + base, :H])


def incoming_half(l_ref, r_ref, write):
    total = nt_dot(l_ref[...], r_ref[...]).astype(BF16)
    for c in range(8):
        for q in range(4):
            part = total[c * T : (c + 1) * T, q * 128 : (q + 1) * 128]
            first, second = sides(part[:H], part[H:])
            write(c, q, first)
            write(c, 8 + q, second)


def incoming_own_kernel(x_ref, l_ref, r_ref, half_ref):
    for c in range(8):
        base = (c % 2) * 8 + c // 2
        for q in range(8):
            cols = slice(q * 128, (q + 1) * 128)
            spread_rows(r_ref, c * T, cols, x_ref[16 * q + base, H:], x_ref[16 * q + 4 + base, H:])

    def write(plane, base, value):
        half_ref[plane * 8 + base // 8 * 4 + base % 4] = value

    incoming_half(l_ref, r_ref, write)


def incoming_sum_kernel(l_ref, r_ref, half_ref, y_ref):
    own = lax.axis_index("core")

    def write(plane, base, value):
        y_ref[plane * 16 + (1 - own) * 4 + base] = value

    incoming_half(l_ref, r_ref, write)
    for plane in range(8):
        for y in range(2):
            y_ref[pl.ds(plane * 16 + y * 8 + own * 4, 4)] = half_ref[plane * 8 + y * 4 : plane * 8 + y * 4 + 4]


def call(kernel, outs, scratch=(), specs=None, out_specs=None, limit=VMEM_LIMIT):
    return pl.pallas_call(
        kernel,
        out_shape=[jax.ShapeDtypeStruct(s, d) for s, d in outs],
        scratch_shapes=[pltpu.VMEM(*m) if isinstance(m, tuple) else m for m in scratch],
        compiler_params=pltpu.CompilerParams(vmem_limit_bytes=limit),
        **({} if specs is None else {"in_specs": specs}),
        **({} if out_specs is None else {"out_specs": out_specs}),
    )


VMEM_SPEC = pl.BlockSpec(memory_space=pltpu.VMEM)
SMEM_SPEC = pl.BlockSpec(memory_space=pltpu.SMEM)
HBM_SPEC = pl.BlockSpec(memory_space=pltpu.HBM)
CHIPS = ("z", "yh", "yl", "x")
SWAP = ((0, 1), (1, 0))


def exchange(x):
    return lax.all_to_all(x, CHIPS, split_axis=0, concat_axis=0, tiled=True)


def on_device(
    pair, token_mask, in_gain, in_bias, proj_weight, gate_weight, mid_gain, mid_bias, out_weight
):
    mask = token_mask[None]
    gates = ((H, 2 * T, C), F32)
    wide = ((C, T, 2 * T), BF16)
    narrow = ((C, H, 2 * T), BF16)
    line = (((C + 1) * PITCH, 2 * T), F32)
    tile = (((T + 1) * WIDE, C), F32)

    x, gate0 = call(
        first_kernel,
        [wide, gates],
        [
            line, line, ((T, T, C), F32), pltpu.SMEM((1024,), jnp.int32), ((1, 1024), jnp.int32), ((2, C), F32),
            ((2, C), F32), ((C, 4 * C), BF16), ((C, C), BF16), wide, gates, pltpu.SemaphoreType.DMA((6,)),
            pltpu.SemaphoreType.DMA((T // BLK,)), pltpu.SemaphoreType.DMA((6,)),
        ],
        [HBM_SPEC] * 7,
        [HBM_SPEC] * 2,
        FIRST_LIMIT,
    )(
        pair, token_mask, mask, in_gain, in_bias, proj_weight, gate_weight
    )
    x = exchange(x)
    right = ((512, 512), BF16)
    left, other = call(outgoing_other_kernel, [((1024, 512), BF16), ((1024, 512), BF16)], [right])(x)
    got = lax.ppermute(other, "core", SWAP)
    (own,) = call(outgoing_own_kernel, [((1024, 512), F32)], [right])(x, left)
    (y,) = call(outgoing_sum_kernel, [narrow])(own, got)
    y = exchange(y)
    x, gate1, current = call(middle_kernel, [wide, tile, tile], [line, line], [VMEM_SPEC] * 6 + [SMEM_SPEC] + [VMEM_SPEC] * 5)(
        y, pair, gate0, mid_gain, mid_bias, out_weight,
        token_mask, mask, in_gain, in_bias, proj_weight, gate_weight,
    )
    x = exchange(x)
    side = ((512, 1024), BF16)
    (left,) = call(incoming_left_kernel, [side])(x)
    got = lax.ppermute(left, "core", SWAP)
    right, half = call(incoming_own_kernel, [side, ((64, H, 2 * T), BF16)])(x, left)
    (y,) = call(incoming_sum_kernel, [narrow])(got, right, half)
    y = exchange(y)
    (out,) = call(
        last_kernel,
        [((T, T, C), F32)],
        [line, ((T, T, C), F32), pltpu.SemaphoreType.DMA((4,))],
        [VMEM_SPEC] * 6,
        [HBM_SPEC],
    )(
        y, current, gate1, mid_gain, mid_bias, out_weight
    )
    return out


def solution(mesh):
    inner = jax.sharding.Mesh(mesh.devices.reshape(8, 2, 4, 2, 2), ("z", "yl", "x", "yh", "core"))
    spec = P(("z", "yl"), ("x", "yh", "core"), None)
    return jax.shard_map(
        on_device,
        mesh=inner,
        in_specs=(spec, P(), P(), P(), P(), P(), P(), P(), P()),
        out_specs=spec,
        check_vma=False,
    )
```

```python
import jax
import jax.numpy as jnp
from jax import lax
from jax.experimental import pallas as pl
from jax.experimental.pallas import tpu as pltpu
from jax.sharding import PartitionSpec as P

F32 = jnp.float32
BF16 = jnp.bfloat16
C = 128
T = 64
H = 32
PITCH = 24
WIDE = 72
BLK = 16
VMEM_LIMIT = 24 * 1024 * 1024
FIRST_LIMIT = 56 * 1024 * 1024


def halved(weights):
    return (weights.astype(F32) * 0.5).astype(BF16)


def gate_weights_halved(w):
    blocks = [w[:, i * C : (i + 1) * C] for i in range(4)]
    return jnp.concatenate([halved(blocks[0]), blocks[1], halved(blocks[2]), blocks[3]], axis=1)


def layer_norm(values, gain, bias):
    average = jnp.mean(values, axis=-1, keepdims=True)
    centred = values - average
    spread = jnp.mean(centred * centred, axis=-1, keepdims=True)
    return centred * lax.rsqrt(spread + 1e-05) * gain + bias


def lanes_twice(mask_ref, block):
    chunk = mask_ref[:, pl.ds(pl.multiple_of(lax.div(block, 2) * 2 * T, 2 * T), 2 * T)].astype(F32)
    turned = jnp.concatenate([chunk[:, T:], chunk[:, :T]], axis=1)
    lane = lax.broadcasted_iota(jnp.int32, (1, 2 * T), 1)
    keep = lax.div(lane, T) == lax.rem(block, 2)
    return jnp.where(keep, chunk, turned) * 0.5


def line_mask(token_ref, start, s, across):
    lane = lax.broadcasted_iota(jnp.int32, (1, 2 * T), 1)
    first, second = token_ref[start + s].astype(F32), token_ref[start + s + H].astype(F32)
    return jnp.where(lane < T, first, second) * across


def row_block():
    return lax.axis_index("z") * 2 + lax.axis_index("yl")


def col_block():
    return lax.axis_index("x") * 4 + lax.axis_index("yh") * 2 + lax.axis_index("core")


def column(row):
    shape = (C, C)
    eye = lax.broadcasted_iota(jnp.int32, shape, 0) == lax.broadcasted_iota(jnp.int32, shape, 1)
    return jnp.sum(jnp.where(eye, jnp.broadcast_to(row, shape), 0.0), axis=1, keepdims=True)


def unpad(ref):
    return ref[: C * PITCH].reshape(C, PITCH, C)[:, :BLK].astype(BF16)


def project_block(load, block, mask, gain, bias, w, g, x_ref, keep_gate, sl_ref, sr_ref):
    for t in range(0, BLK, 2):
        s = block * BLK + t
        lines = jnp.concatenate([load(s), load(s + H), load(s + 1), load(s + 1 + H)], axis=0)
        normed = layer_norm(lines, gain, bias).astype(BF16)
        p = lax.dot_general(
            w, normed, (((0,), (1,)), ((), ())), preferred_element_type=F32
        )
        if keep_gate is not None:
            gate = jnp.tanh(jnp.dot(normed, g, preferred_element_type=F32)) + 1.0
            keep_gate(s, gate[:C])
            keep_gate(s + 1, gate[C:])
        left = (jnp.tanh(p[:C]) + 1.0) * p[C : 2 * C]
        right = (jnp.tanh(p[2 * C : 3 * C]) + 1.0) * p[3 * C :]
        for u in range(2):
            keep = mask(s + u)
            sl_ref[pl.ds(t + u, C, stride=PITCH), :] = left[:, u * C : (u + 1) * C] * keep
            sr_ref[pl.ds(t + u, C, stride=PITCH), :] = right[:, u * C : (u + 1) * C] * keep
    x_ref[:, pl.ds(pl.multiple_of(block * BLK, BLK), BLK), :] = unpad(sl_ref)
    x_ref[:, pl.ds(pl.multiple_of(H + block * BLK, BLK), BLK), :] = unpad(sr_ref)


def first_kernel(
    z_hbm, token_hbm, mask_hbm, gain_hbm, bias_hbm, w_hbm, x_hbm, sl_ref, sr_ref,
    z_ref, token_ref, mask_ref, gain_ref, bias_ref, w_ref, x_ref, small_sem, z_sem, out_sem,
):
    small = [
        pltpu.make_async_copy(source, to, small_sem.at[n])
        for n, (source, to) in enumerate(
            (
                (gain_hbm, gain_ref), (bias_hbm, bias_ref), (mask_hbm, mask_ref), (token_hbm, token_ref),
                (w_hbm.at[0], w_ref),
            )
        )
    ]
    parts = []
    for n in range(T // BLK):
        lines = pl.ds(n % 2 * H + n // 2 * BLK, BLK)
        parts.append(pltpu.make_async_copy(z_hbm.at[lines], z_ref.at[lines], z_sem.at[n]))
    for copy in parts[:2] + small + parts[2:]:
        copy.start()
    for copy in small:
        copy.wait()
    gain, bias = gain_ref[0:1], bias_ref[0:1]
    across = lanes_twice(mask_ref, col_block())
    start = row_block() * T
    w = gate_weights_halved(w_ref[...])
    copies = []

    def send(source, to):
        copies.append(pltpu.make_async_copy(source, to, out_sem.at[len(copies)]))
        copies[-1].start()

    for block in range(H // BLK):
        parts[2 * block].wait()
        parts[2 * block + 1].wait()
        project_block(
            lambda s: z_ref[s], block, lambda s: line_mask(token_ref, start, s, across), gain, bias,
            w, None, x_ref, None, sl_ref, sr_ref,
        )
        for half in range(2):
            lines = pl.ds(half * H + block * BLK, BLK)
            send(x_ref.at[:, lines], x_hbm.at[:, lines])
    for copy in copies:
        copy.wait()


def gate_kernel(z_ref, gain_ref, bias_ref, g_ref, gate_ref):
    gain, bias, g = gain_ref[0:1], bias_ref[0:1], halved(g_ref[0])
    for s in range(0, H, 2):
        lines = jnp.concatenate([z_ref[s], z_ref[s + H], z_ref[s + 1], z_ref[s + 1 + H]], axis=0)
        normed = layer_norm(lines, gain, bias).astype(BF16)
        gate = jnp.tanh(jnp.dot(normed, g, preferred_element_type=F32)) + 1.0
        gate_ref[s] = gate[:C]
        gate_ref[s + 1] = gate[C:]


def update_block(block, y_ref, gain, bias, ow, s_ref, emit):
    y = y_ref[:, pl.ds(pl.multiple_of(block * BLK, BLK), BLK), :].astype(F32)
    average = jnp.sum(y, axis=0) * (1.0 / C)
    centred = y - average[None]
    spread = jnp.sum(centred * centred, axis=0) * (1.0 / C)
    s_ref[: C * BLK] = (centred * lax.rsqrt(spread + 1e-05)[None]).reshape(C * BLK, C)
    for t in range(0, BLK, 4):
        lines = jnp.concatenate([s_ref[pl.ds(t + u, C, stride=BLK), :] for u in range(4)], axis=1)
        normed = (lines * gain + bias).astype(BF16)
        update = lax.dot_general(normed, ow, (((0,), (0,)), ((), ())), preferred_element_type=F32)
        for u in range(4):
            s = block * BLK + t + u
            emit(s, update[u * C : (u + 1) * C])


def middle_kernel(
    y_ref, z_ref, gate0_ref, mgain_ref, mbias_ref, ow_ref, token_ref, mask_ref, gain_ref, bias_ref,
    w_ref, g_ref, x_ref, gate_ref, zp_ref, sl_ref, sr_ref,
):
    mgain, mbias = column(mgain_ref[0:1]), column(mbias_ref[0:1])
    gain, bias = gain_ref[1:2], bias_ref[1:2]
    across = lanes_twice(mask_ref, row_block())
    start = col_block() * T
    w, g = gate_weights_halved(w_ref[1]), halved(g_ref[1])

    def keep_gate(s, value):
        gate_ref[pl.ds(s, T, stride=WIDE), :] = value[:T]
        gate_ref[pl.ds(s + H, T, stride=WIDE), :] = value[T:]

    def emit(s, update):
        change = gate0_ref[s] * update
        for i, part in ((s, change[:T]), (s + H, change[T:])):
            zp_ref[pl.ds(pl.multiple_of(i * WIDE, 8), T), :] = z_ref[i] + part

    for block in range(H // BLK):
        update_block(block, y_ref, mgain, mbias, halved(ow_ref[0]), sl_ref, emit)
    for block in range(H // BLK):
        project_block(
            lambda s: zp_ref[pl.ds(s, T, stride=WIDE), :], block, lambda s: line_mask(token_ref, start, s, across), gain, bias,
            w, g, x_ref, keep_gate, sl_ref, sr_ref,
        )


def last_kernel(y_ref, z_ref, gate_ref, mgain_ref, mbias_ref, ow_ref, out_hbm, s_ref, out_ref, sem):
    mgain, mbias = column(mgain_ref[1:2]), column(mbias_ref[1:2])

    def emit(s, update):
        for i, part in ((s, update[:T]), (s + H, update[T:])):
            rows = slice(i * WIDE, i * WIDE + T)
            out_ref[i] = z_ref[rows, :] + gate_ref[rows, :] * part

    copies = []
    for block in range(H // BLK):
        update_block(block, y_ref, mgain, mbias, halved(ow_ref[1]), s_ref, emit)
        for half in range(2):
            lines = pl.ds(half * H + block * BLK, BLK)
            copies.append(pltpu.make_async_copy(out_ref.at[lines], out_hbm.at[lines], sem.at[len(copies)]))
            copies[-1].start()
    for copy in copies:
        copy.wait()


def sides(x0, x1):
    low = jnp.concatenate([x0[:, :T], x1[:, :T]], axis=1)
    high = jnp.concatenate([x0[:, T:], x1[:, T:]], axis=1)
    return low, high


def nt_dot(a, b):
    return lax.dot_general(a, b, (((1,), (1,)), ((), ())), preferred_element_type=F32)


def chip(row, col):
    return lax.div(row, 2) * 16 + lax.rem(col, 2) * 8 + lax.rem(row, 2) * 4 + lax.div(col, 2)


def spread_rows(to_ref, at, cols, x0, x1):
    low, high = sides(x0, x1)
    to_ref[pl.ds(at, H), cols] = low
    to_ref[pl.ds(at + H, H), cols] = high


def gather_right(x_ref, parity, to_ref):
    for m in range(8):
        for q in range(4):
            base = m * 16 + parity * 4 + q
            spread_rows(to_ref, m * T, slice(q * 128, (q + 1) * 128), x_ref[base, H:], x_ref[base + 8, H:])


def outgoing_other_kernel(x_ref, l_ref, other_ref, rs_ref):
    gather_right(x_ref, 1 - lax.axis_index("core"), rs_ref)
    for row in range(16):
        for q in range(4):
            base = (row // 2) * 16 + (row % 2) * 4 + q
            spread_rows(l_ref, row * T, slice(q * 128, (q + 1) * 128), x_ref[base, :H], x_ref[base + 8, :H])
    for i in range(2):
        rows = slice(i * 512, (i + 1) * 512)
        other_ref[rows, :] = nt_dot(l_ref[rows, :], rs_ref[...]).astype(BF16)


def outgoing_own_kernel(x_ref, l_ref, own_ref, rs_ref):
    gather_right(x_ref, lax.axis_index("core"), rs_ref)
    for i in range(2):
        rows = slice(i * 512, (i + 1) * 512)
        own_ref[rows, :] = nt_dot(l_ref[rows, :], rs_ref[...])


def outgoing_sum_kernel(own_ref, got_ref, y_ref):
    for row in range(16):
        rows = slice(row * T, (row + 1) * T)
        total = (own_ref[rows, :] + got_ref[rows, :].astype(F32)).astype(BF16)
        base = (row // 2) * 16 + (row % 2) * 4
        for q in range(4):
            part = total[:, q * 128 : (q + 1) * 128]
            first, second = sides(part[:H], part[H:])
            y_ref[base + q] = first
            y_ref[base + 8 + q] = second


def incoming_left_kernel(x_ref, l_ref):
    for c in range(8):
        base = (c % 2) * 8 + c // 2
        for q in range(8):
            cols = slice(q * 128, (q + 1) * 128)
            spread_rows(l_ref, c * T, cols, x_ref[16 * q + base, :H], x_ref[16 * q + 4 + base, :H])


def incoming_half(l_ref, r_ref, write):
    total = nt_dot(l_ref[...], r_ref[...]).astype(BF16)
    for c in range(8):
        for q in range(4):
            part = total[c * T : (c + 1) * T, q * 128 : (q + 1) * 128]
            first, second = sides(part[:H], part[H:])
            write(c, q, first)
            write(c, 8 + q, second)


def incoming_own_kernel(x_ref, l_ref, r_ref, half_ref):
    for c in range(8):
        base = (c % 2) * 8 + c // 2
        for q in range(8):
            cols = slice(q * 128, (q + 1) * 128)
            spread_rows(r_ref, c * T, cols, x_ref[16 * q + base, H:], x_ref[16 * q + 4 + base, H:])

    def write(plane, base, value):
        half_ref[plane * 8 + base // 8 * 4 + base % 4] = value

    incoming_half(l_ref, r_ref, write)


def incoming_sum_kernel(l_ref, r_ref, half_ref, y_ref):
    own = lax.axis_index("core")

    def write(plane, base, value):
        y_ref[plane * 16 + (1 - own) * 4 + base] = value

    incoming_half(l_ref, r_ref, write)
    for plane in range(8):
        for y in range(2):
            y_ref[pl.ds(plane * 16 + y * 8 + own * 4, 4)] = half_ref[plane * 8 + y * 4 : plane * 8 + y * 4 + 4]


def call(kernel, outs, scratch=(), specs=None, out_specs=None, limit=VMEM_LIMIT):
    return pl.pallas_call(
        kernel,
        out_shape=[jax.ShapeDtypeStruct(s, d) for s, d in outs],
        scratch_shapes=[pltpu.VMEM(*m) if isinstance(m, tuple) else m for m in scratch],
        compiler_params=pltpu.CompilerParams(vmem_limit_bytes=limit),
        **({} if specs is None else {"in_specs": specs}),
        **({} if out_specs is None else {"out_specs": out_specs}),
    )


VMEM_SPEC = pl.BlockSpec(memory_space=pltpu.VMEM)
SMEM_SPEC = pl.BlockSpec(memory_space=pltpu.SMEM)
HBM_SPEC = pl.BlockSpec(memory_space=pltpu.HBM)
CHIPS = ("z", "yh", "yl", "x")
SWAP = ((0, 1), (1, 0))


def exchange(x):
    return lax.all_to_all(x, CHIPS, split_axis=0, concat_axis=0, tiled=True)


def on_device(
    pair, token_mask, in_gain, in_bias, proj_weight, gate_weight, mid_gain, mid_bias, out_weight
):
    mask = token_mask[None]
    gates = ((H, 2 * T, C), F32)
    wide = ((C, T, 2 * T), BF16)
    narrow = ((C, H, 2 * T), BF16)
    line = (((C + 1) * PITCH, 2 * T), F32)
    tile = (((T + 1) * WIDE, C), F32)

    (x,) = call(
        first_kernel,
        [wide],
        [
            line, line, ((T, T, C), F32), pltpu.SMEM((1024,), jnp.int32), ((1, 1024), jnp.int32), ((2, C), F32),
            ((2, C), F32), ((C, 4 * C), BF16), wide, pltpu.SemaphoreType.DMA((5,)),
            pltpu.SemaphoreType.DMA((T // BLK,)), pltpu.SemaphoreType.DMA((4,)),
        ],
        [HBM_SPEC] * 6,
        [HBM_SPEC],
        FIRST_LIMIT,
    )(
        pair, token_mask, mask, in_gain, in_bias, proj_weight
    )
    x = exchange(x)
    right = ((512, 512), BF16)
    left, other = call(outgoing_other_kernel, [((1024, 512), BF16), ((1024, 512), BF16)], [right])(x)
    got = lax.ppermute(other, "core", SWAP)
    later = lax.optimization_barrier((pair, other))[0]
    (gate0,) = call(gate_kernel, [gates])(later, in_gain, in_bias, gate_weight)
    (own,) = call(outgoing_own_kernel, [((1024, 512), F32)], [right])(x, left)
    (y,) = call(outgoing_sum_kernel, [narrow])(own, got)
    y = exchange(y)
    x, gate1, current = call(middle_kernel, [wide, tile, tile], [line, line], [VMEM_SPEC] * 6 + [SMEM_SPEC] + [VMEM_SPEC] * 5)(
        y, pair, gate0, mid_gain, mid_bias, out_weight,
        token_mask, mask, in_gain, in_bias, proj_weight, gate_weight,
    )
    x = exchange(x)
    side = ((512, 1024), BF16)
    (left,) = call(incoming_left_kernel, [side])(x)
    got = lax.ppermute(left, "core", SWAP)
    right, half = call(incoming_own_kernel, [side, ((64, H, 2 * T), BF16)])(x, left)
    (y,) = call(incoming_sum_kernel, [narrow])(got, right, half)
    y = exchange(y)
    (out,) = call(
        last_kernel,
        [((T, T, C), F32)],
        [line, ((T, T, C), F32), pltpu.SemaphoreType.DMA((4,))],
        [VMEM_SPEC] * 6,
        [HBM_SPEC],
    )(
        y, current, gate1, mid_gain, mid_bias, out_weight
    )
    return out


def solution(mesh):
    inner = jax.sharding.Mesh(mesh.devices.reshape(8, 2, 4, 2, 2), ("z", "yl", "x", "yh", "core"))
    spec = P(("z", "yl"), ("x", "yh", "core"), None)
    return jax.shard_map(
        on_device,
        mesh=inner,
        in_specs=(spec, P(), P(), P(), P(), P(), P(), P(), P()),
        out_specs=spec,
        check_vma=False,
    )
```

```python
import jax
import jax.numpy as jnp
from jax import lax
from jax.experimental import pallas as pl
from jax.experimental.pallas import tpu as pltpu
from jax.sharding import PartitionSpec as P

F32 = jnp.float32
BF16 = jnp.bfloat16
C = 128
T = 64
H = 32
PITCH = 24
WIDE = 72
BLK = 16
VMEM_LIMIT = 24 * 1024 * 1024
FIRST_LIMIT = 56 * 1024 * 1024


def halved(weights):
    return (weights.astype(F32) * 0.5).astype(BF16)


def gate_weights_halved(w):
    blocks = [w[:, i * C : (i + 1) * C] for i in range(4)]
    return jnp.concatenate([halved(blocks[0]), blocks[1], halved(blocks[2]), blocks[3]], axis=1)


def layer_norm(values, gain, bias):
    average = jnp.mean(values, axis=-1, keepdims=True)
    centred = values - average
    spread = jnp.mean(centred * centred, axis=-1, keepdims=True)
    return centred * lax.rsqrt(spread + 1e-05) * gain + bias


def lanes_twice(mask_ref, block):
    chunk = mask_ref[:, pl.ds(pl.multiple_of(lax.div(block, 2) * 2 * T, 2 * T), 2 * T)].astype(F32)
    turned = jnp.concatenate([chunk[:, T:], chunk[:, :T]], axis=1)
    lane = lax.broadcasted_iota(jnp.int32, (1, 2 * T), 1)
    keep = lax.div(lane, T) == lax.rem(block, 2)
    return jnp.where(keep, chunk, turned) * 0.5


def line_mask(token_ref, start, s, across):
    lane = lax.broadcasted_iota(jnp.int32, (1, 2 * T), 1)
    first, second = token_ref[start + s].astype(F32), token_ref[start + s + H].astype(F32)
    return jnp.where(lane < T, first, second) * across


def row_block():
    return lax.axis_index("z") * 2 + lax.axis_index("yl")


def col_block():
    return lax.axis_index("x") * 4 + lax.axis_index("yh") * 2 + lax.axis_index("core")


def column(row):
    shape = (C, C)
    eye = lax.broadcasted_iota(jnp.int32, shape, 0) == lax.broadcasted_iota(jnp.int32, shape, 1)
    return jnp.sum(jnp.where(eye, jnp.broadcast_to(row, shape), 0.0), axis=1, keepdims=True)


def unpad(ref):
    return ref[: C * PITCH].reshape(C, PITCH, C)[:, :BLK].astype(BF16)


def project_block(load, block, mask, gain, bias, w, g, x_ref, keep_gate, sl_ref, sr_ref):
    for t in range(0, BLK, 4):
        s = block * BLK + t
        lines = jnp.concatenate([load(s + u + h) for u in range(4) for h in (0, H)], axis=0)
        normed = layer_norm(lines, gain, bias).astype(BF16)
        p = lax.dot_general(w, normed, (((0,), (1,)), ((), ())), preferred_element_type=F32)
        gate = jnp.tanh(jnp.dot(normed, g, preferred_element_type=F32)) + 1.0
        left = (jnp.tanh(p[:C]) + 1.0) * p[C : 2 * C]
        right = (jnp.tanh(p[2 * C : 3 * C]) + 1.0) * p[3 * C :]
        for u in range(4):
            keep = mask(s + u)
            keep_gate(s + u, gate[u * C : (u + 1) * C])
            sl_ref[pl.ds(t + u, C, stride=PITCH), :] = left[:, u * C : (u + 1) * C] * keep
            sr_ref[pl.ds(t + u, C, stride=PITCH), :] = right[:, u * C : (u + 1) * C] * keep
    x_ref[:, pl.ds(pl.multiple_of(block * BLK, BLK), BLK), :] = unpad(sl_ref)
    x_ref[:, pl.ds(pl.multiple_of(H + block * BLK, BLK), BLK), :] = unpad(sr_ref)


def first_kernel(
    z_hbm, token_hbm, mask_hbm, gain_hbm, bias_hbm, w_hbm, g_hbm, x_hbm, gate_hbm, sl_ref, sr_ref,
    z_ref, token_ref, mask_ref, gain_ref, bias_ref, w_ref, g_ref, x_ref, gate_ref, small_sem, z_sem, out_sem,
):
    small = [
        pltpu.make_async_copy(source, to, small_sem.at[n])
        for n, (source, to) in enumerate(
            (
                (gain_hbm, gain_ref), (bias_hbm, bias_ref), (mask_hbm, mask_ref), (token_hbm, token_ref),
                (w_hbm.at[0], w_ref), (g_hbm.at[0], g_ref),
            )
        )
    ]
    parts = []
    for n in range(T // BLK):
        lines = pl.ds(n % 2 * H + n // 2 * BLK, BLK)
        parts.append(pltpu.make_async_copy(z_hbm.at[lines], z_ref.at[lines], z_sem.at[n]))
    for copy in parts[:2] + small + parts[2:]:
        copy.start()
    for copy in small:
        copy.wait()
    gain, bias = gain_ref[0:1], bias_ref[0:1]
    across = lanes_twice(mask_ref, col_block())
    start = row_block() * T
    w, g = gate_weights_halved(w_ref[...]), halved(g_ref[...])
    copies = []

    def keep_gate(s, value):
        gate_ref[s] = value

    def send(source, to):
        copies.append(pltpu.make_async_copy(source, to, out_sem.at[len(copies)]))
        copies[-1].start()

    for block in range(H // BLK):
        parts[2 * block].wait()
        parts[2 * block + 1].wait()
        project_block(
            lambda s: z_ref[s], block, lambda s: line_mask(token_ref, start, s, across), gain, bias,
            w, g, x_ref, keep_gate, sl_ref, sr_ref,
        )
        for half in range(2):
            lines = pl.ds(half * H + block * BLK, BLK)
            send(x_ref.at[:, lines], x_hbm.at[:, lines])
        lines = pl.ds(block * BLK, BLK)
        send(gate_ref.at[lines], gate_hbm.at[lines])
    for copy in copies:
        copy.wait()


def update_block(block, y_ref, gain, bias, ow, s_ref, emit):
    y = y_ref[:, pl.ds(pl.multiple_of(block * BLK, BLK), BLK), :].astype(F32)
    average = jnp.sum(y, axis=0) * (1.0 / C)
    centred = y - average[None]
    spread = jnp.sum(centred * centred, axis=0) * (1.0 / C)
    s_ref[: C * BLK] = (centred * lax.rsqrt(spread + 1e-05)[None]).reshape(C * BLK, C)
    for t in range(0, BLK, 4):
        lines = jnp.concatenate([s_ref[pl.ds(t + u, C, stride=BLK), :] for u in range(4)], axis=1)
        normed = (lines * gain + bias).astype(BF16)
        update = lax.dot_general(normed, ow, (((0,), (0,)), ((), ())), preferred_element_type=F32)
        for u in range(4):
            s = block * BLK + t + u
            emit(s, update[u * C : (u + 1) * C])


def middle_kernel(
    y_ref, z_ref, gate0_ref, mgain_ref, mbias_ref, ow_ref, token_ref, mask_ref, gain_ref, bias_ref,
    w_ref, g_ref, x_ref, gate_ref, zp_ref, sl_ref, sr_ref,
):
    mgain, mbias = column(mgain_ref[0:1]), column(mbias_ref[0:1])
    gain, bias = gain_ref[1:2], bias_ref[1:2]
    across = lanes_twice(mask_ref, row_block())
    start = col_block() * T
    w, g = gate_weights_halved(w_ref[1]), halved(g_ref[1])

    def keep_gate(s, value):
        gate_ref[pl.ds(s, T, stride=WIDE), :] = value[:T]
        gate_ref[pl.ds(s + H, T, stride=WIDE), :] = value[T:]

    def emit(s, update):
        change = gate0_ref[s] * update
        for i, part in ((s, change[:T]), (s + H, change[T:])):
            zp_ref[pl.ds(pl.multiple_of(i * WIDE, 8), T), :] = z_ref[i] + part

    for block in range(H // BLK):
        update_block(block, y_ref, mgain, mbias, halved(ow_ref[0]), sl_ref, emit)
    for block in range(H // BLK):
        project_block(
            lambda s: zp_ref[pl.ds(s, T, stride=WIDE), :], block, lambda s: line_mask(token_ref, start, s, across), gain, bias,
            w, g, x_ref, keep_gate, sl_ref, sr_ref,
        )


def last_kernel(y_ref, z_ref, gate_ref, mgain_ref, mbias_ref, ow_ref, out_hbm, s_ref, out_ref, sem):
    mgain, mbias = column(mgain_ref[1:2]), column(mbias_ref[1:2])

    def emit(s, update):
        for i, part in ((s, update[:T]), (s + H, update[T:])):
            rows = slice(i * WIDE, i * WIDE + T)
            out_ref[i] = z_ref[rows, :] + gate_ref[rows, :] * part

    copies = []
    for block in range(H // BLK):
        update_block(block, y_ref, mgain, mbias, halved(ow_ref[1]), s_ref, emit)
        for half in range(2):
            lines = pl.ds(half * H + block * BLK, BLK)
            copies.append(pltpu.make_async_copy(out_ref.at[lines], out_hbm.at[lines], sem.at[len(copies)]))
            copies[-1].start()
    for copy in copies:
        copy.wait()


def sides(x0, x1):
    low = jnp.concatenate([x0[:, :T], x1[:, :T]], axis=1)
    high = jnp.concatenate([x0[:, T:], x1[:, T:]], axis=1)
    return low, high


def nt_dot(a, b):
    return lax.dot_general(a, b, (((1,), (1,)), ((), ())), preferred_element_type=F32)


def chip(row, col):
    return lax.div(row, 2) * 16 + lax.rem(col, 2) * 8 + lax.rem(row, 2) * 4 + lax.div(col, 2)


def spread_rows(to_ref, at, cols, x0, x1):
    low, high = sides(x0, x1)
    to_ref[pl.ds(at, H), cols] = low
    to_ref[pl.ds(at + H, H), cols] = high


def gather_right(x_ref, parity, to_ref):
    for m in range(8):
        for q in range(4):
            base = m * 16 + parity * 4 + q
            spread_rows(to_ref, m * T, slice(q * 128, (q + 1) * 128), x_ref[base, H:], x_ref[base + 8, H:])


def outgoing_other_kernel(x_ref, l_ref, other_ref, rs_ref):
    gather_right(x_ref, 1 - lax.axis_index("core"), rs_ref)
    for row in range(16):
        for q in range(4):
            base = (row // 2) * 16 + (row % 2) * 4 + q
            spread_rows(l_ref, row * T, slice(q * 128, (q + 1) * 128), x_ref[base, :H], x_ref[base + 8, :H])
    for i in range(2):
        rows = slice(i * 512, (i + 1) * 512)
        other_ref[rows, :] = nt_dot(l_ref[rows, :], rs_ref[...]).astype(BF16)


def outgoing_own_kernel(x_ref, l_ref, own_ref, rs_ref):
    gather_right(x_ref, lax.axis_index("core"), rs_ref)
    for i in range(2):
        rows = slice(i * 512, (i + 1) * 512)
        own_ref[rows, :] = nt_dot(l_ref[rows, :], rs_ref[...])


def outgoing_sum_kernel(own_ref, got_ref, y_ref):
    for row in range(16):
        rows = slice(row * T, (row + 1) * T)
        total = (own_ref[rows, :] + got_ref[rows, :].astype(F32)).astype(BF16)
        base = (row // 2) * 16 + (row % 2) * 4
        for q in range(4):
            part = total[:, q * 128 : (q + 1) * 128]
            first, second = sides(part[:H], part[H:])
            y_ref[base + q] = first
            y_ref[base + 8 + q] = second


def incoming_left_kernel(x_ref, l_ref):
    for c in range(8):
        base = (c % 2) * 8 + c // 2
        for q in range(8):
            cols = slice(q * 128, (q + 1) * 128)
            spread_rows(l_ref, c * T, cols, x_ref[16 * q + base, :H], x_ref[16 * q + 4 + base, :H])


def incoming_half(l_ref, r_ref, write):
    total = nt_dot(l_ref[...], r_ref[...]).astype(BF16)
    for c in range(8):
        for q in range(4):
            part = total[c * T : (c + 1) * T, q * 128 : (q + 1) * 128]
            first, second = sides(part[:H], part[H:])
            write(c, q, first)
            write(c, 8 + q, second)


def incoming_own_kernel(x_ref, l_ref, r_ref, half_ref):
    for c in range(8):
        base = (c % 2) * 8 + c // 2
        for q in range(8):
            cols = slice(q * 128, (q + 1) * 128)
            spread_rows(r_ref, c * T, cols, x_ref[16 * q + base, H:], x_ref[16 * q + 4 + base, H:])

    def write(plane, base, value):
        half_ref[plane * 8 + base // 8 * 4 + base % 4] = value

    incoming_half(l_ref, r_ref, write)


def incoming_sum_kernel(l_ref, r_ref, half_ref, y_ref):
    own = lax.axis_index("core")

    def write(plane, base, value):
        y_ref[plane * 16 + (1 - own) * 4 + base] = value

    incoming_half(l_ref, r_ref, write)
    for plane in range(8):
        for y in range(2):
            y_ref[pl.ds(plane * 16 + y * 8 + own * 4, 4)] = half_ref[plane * 8 + y * 4 : plane * 8 + y * 4 + 4]


def call(kernel, outs, scratch=(), specs=None, out_specs=None, limit=VMEM_LIMIT):
    return pl.pallas_call(
        kernel,
        out_shape=[jax.ShapeDtypeStruct(s, d) for s, d in outs],
        scratch_shapes=[pltpu.VMEM(*m) if isinstance(m, tuple) else m for m in scratch],
        compiler_params=pltpu.CompilerParams(vmem_limit_bytes=limit),
        **({} if specs is None else {"in_specs": specs}),
        **({} if out_specs is None else {"out_specs": out_specs}),
    )


VMEM_SPEC = pl.BlockSpec(memory_space=pltpu.VMEM)
SMEM_SPEC = pl.BlockSpec(memory_space=pltpu.SMEM)
HBM_SPEC = pl.BlockSpec(memory_space=pltpu.HBM)
CHIPS = ("z", "yh", "yl", "x")
SWAP = ((0, 1), (1, 0))


def exchange(x):
    return lax.all_to_all(x, CHIPS, split_axis=0, concat_axis=0, tiled=True)


def on_device(
    pair, token_mask, in_gain, in_bias, proj_weight, gate_weight, mid_gain, mid_bias, out_weight
):
    mask = token_mask[None]
    gates = ((H, 2 * T, C), F32)
    wide = ((C, T, 2 * T), BF16)
    narrow = ((C, H, 2 * T), BF16)
    line = (((C + 1) * PITCH, 2 * T), F32)
    tile = (((T + 1) * WIDE, C), F32)

    x, gate0 = call(
        first_kernel,
        [wide, gates],
        [
            line, line, ((T, T, C), F32), pltpu.SMEM((1024,), jnp.int32), ((1, 1024), jnp.int32), ((2, C), F32),
            ((2, C), F32), ((C, 4 * C), BF16), ((C, C), BF16), wide, gates, pltpu.SemaphoreType.DMA((6,)),
            pltpu.SemaphoreType.DMA((T // BLK,)), pltpu.SemaphoreType.DMA((6,)),
        ],
        [HBM_SPEC] * 7,
        [HBM_SPEC] * 2,
        FIRST_LIMIT,
    )(
        pair, token_mask, mask, in_gain, in_bias, proj_weight, gate_weight
    )
    x = exchange(x)
    right = ((512, 512), BF16)
    left, other = call(outgoing_other_kernel, [((1024, 512), BF16), ((1024, 512), BF16)], [right])(x)
    got = lax.ppermute(other, "core", SWAP)
    (own,) = call(outgoing_own_kernel, [((1024, 512), F32)], [right])(x, left)
    (y,) = call(outgoing_sum_kernel, [narrow])(own, got)
    y = exchange(y)
    x, gate1, current = call(middle_kernel, [wide, tile, tile], [line, line], [VMEM_SPEC] * 6 + [SMEM_SPEC] + [VMEM_SPEC] * 5)(
        y, pair, gate0, mid_gain, mid_bias, out_weight,
        token_mask, mask, in_gain, in_bias, proj_weight, gate_weight,
    )
    x = exchange(x)
    side = ((512, 1024), BF16)
    (left,) = call(incoming_left_kernel, [side])(x)
    got = lax.ppermute(left, "core", SWAP)
    right, half = call(incoming_own_kernel, [side, ((64, H, 2 * T), BF16)])(x, left)
    (y,) = call(incoming_sum_kernel, [narrow])(got, right, half)
    y = exchange(y)
    (out,) = call(
        last_kernel,
        [((T, T, C), F32)],
        [line, ((T, T, C), F32), pltpu.SemaphoreType.DMA((4,))],
        [VMEM_SPEC] * 6,
        [HBM_SPEC],
    )(
        y, current, gate1, mid_gain, mid_bias, out_weight
    )
    return out


def solution(mesh):
    inner = jax.sharding.Mesh(mesh.devices.reshape(8, 2, 4, 2, 2), ("z", "yl", "x", "yh", "core"))
    spec = P(("z", "yl"), ("x", "yh", "core"), None)
    return jax.shard_map(
        on_device,
        mesh=inner,
        in_specs=(spec, P(), P(), P(), P(), P(), P(), P(), P()),
        out_specs=spec,
        check_vma=False,
    )
```
